512 devices in a mesh: people: 32 (over z, core), var: 16 (over y, x).
Axes of the slice: x: 4, y: 4, z: 16, core: 2. Of those that a mesh axis runs over, the one named last changes fastest.
Arguments:
- genotype: int32 [16384, 16384], P('people', 'var'), may hold values from 0 to 2
- dosage_mean: float32 [16384], P('var'), may hold values from 0.6 to 1.4
- residual: float32 [4, 16384], P(None, 'people'), may hold values from -10.5 to 10.5, as said below
- latent_old: float32 [4, 16, 16384], P(None, 'var'), may hold values from -3 to 3
- group_weight: float32 [2048], P('var'), may hold values from 1 to 40
- copy_source: int32 [16, 16, 1024], P('var'), may hold values from 0 to 1023
- copy_slot: int32 [16, 16, 1024], P('var'), may hold values from -1 to 16383, as said below
Outputs:
- latent_new: float32 [4, 16, 16384], P(None, 'var')
- coef_change: float32 [4, 16384], P(None, 'var')
- residual_new: float32 [4, 16384], P(None, 'people')
The draws below stay inside these ranges and needn't reach their ends.
Inputs may be any that keep to these rules, and one draw needn't show every extreme that they name: Each row is a trait's residual over people, scaled from 1 to 3 along the people. copy_slot[o, s, :] lists the slots (group-major among owner o's 128 groups of 128) filled from slab s; used entries come first and -1 marks the rest; the live entries of one owner are distinct; in each draw some slab fills an owner's whole list of 1024, for every owner, and one owner has all its lists full.
All inputs are finite; a program needn't handle non-finite values.
Results may differ from the reference program's by a relative error of at most 0.00012.
Values sent between devices are 32-bit elements; how exact they have to be, the bound alone decides.
A program may use at most 64 MiB of HBM per device.

```python
import math
import jax
import jax.numpy as jnp
from jax import lax

PEOPLE_DEV = 512
TRAITS = 4
VAR_DEV = 1024
GRP_DEV = 128
GSIZE = 128
CAP = 1024
PEOPLE = 16384
VARIANTS = 16384
GROUPS = 2048
N_PEOPLE = 32
N_VAR = 16


def draw_residual(key, part):
    key = jax.random.fold_in(key, 3)
    rising = 1.0 + 2.0 * jnp.arange(PEOPLE, dtype=jnp.float32) / PEOPLE
    values = jnp.clip(jax.random.normal(key, (TRAITS, PEOPLE), jnp.float32), -3.5, 3.5)
    return (values * rising[None, :]).astype(jnp.float32)


def owner_order(subkey):
    return jax.random.permutation(subkey, GRP_DEV * GSIZE)


def draw_copy_slot(key, part):
    key = jax.random.fold_in(key, 7)
    subkeys = jax.random.split(key, 5)
    slot_count = GRP_DEV * GSIZE
    owners = jnp.arange(N_VAR, dtype=jnp.int32)
    weights = jax.random.randint(subkeys[0], (N_VAR, 1), 1, 5)
    counts = jnp.minimum(CAP, jax.random.randint(subkeys[1], (N_VAR, N_VAR), 0, CAP // 4 + 1) * weights)
    forced = jax.random.randint(subkeys[2], (N_VAR,), 0, N_VAR)
    counts = jnp.where(owners[None, :] == forced[:, None], CAP, counts)
    busiest = jax.random.randint(subkeys[3], (), 0, N_VAR)
    counts = jnp.where(owners[:, None] == busiest, CAP, counts)
    offsets = jnp.cumsum(counts, axis=1) - counts
    places = jnp.arange(CAP, dtype=jnp.int32)
    rank_values = offsets[:, :, None] + places[None, None, :]
    occupied = places[None, None, :] < counts[:, :, None]
    orders = jax.vmap(owner_order)(jax.random.split(subkeys[4], N_VAR))
    chosen = jnp.take_along_axis(orders, jnp.minimum(rank_values, slot_count - 1).reshape(N_VAR, N_VAR * CAP), axis=1)
    return jnp.where(occupied, chosen.reshape(N_VAR, N_VAR, CAP), -1).astype(jnp.int32)


def with_ends(values, rng, low, top_value):
    extent = values.shape
    index_at = [jax.random.randint(jax.random.fold_in(rng, axis), (), 0, extent[axis]) for axis in range(len(extent))]
    values = values.at[tuple(index_at)].set(low)
    longest = extent.index(max(extent))
    index_at[longest] = (index_at[longest] + 1) % extent[longest]
    return values.at[tuple(index_at)].set(top_value)


def shard_levels(rng, extent, cuts, low, top_value):
    def one(position, parts):
        draws = jax.random.uniform(jax.random.fold_in(jax.random.fold_in(rng, 6), position), (parts,), jnp.float32, low / len(cuts), top_value / len(cuts))
        return jnp.repeat(jnp.exp(draws), extent[position] // parts).reshape((-1,) + (1,) * (len(extent) - position - 1))

    gain = one(*cuts[0])
    for cut in cuts[1:]:
        gain = gain * one(*cut)
    return gain


def bell_draw(own_key, extent, spread, most, cuts=(), held_as=jnp.bfloat16):
    drawn = jax.random.normal(own_key, extent, jnp.float32) * spread
    if len(cuts) > 0:
        drawn = shard_levels(own_key, extent, cuts, -0.22, 0.18) * drawn
    return jnp.clip(drawn, min=-most, max=most).astype(held_as)


def setup_inputs(seed: int = 0) -> dict:
    seeds = jax.random.split(jax.random.key(seed), 8)
    genotype = with_ends(jax.random.randint(seeds[0], (PEOPLE, VARIANTS), 0, 3), jax.random.fold_in(seeds[0], 1), 0, 2).astype(jnp.int32)
    dosage_mean = jnp.clip(0.6 + 0.79999995 * jax.random.uniform(seeds[1], (VARIANTS,), jnp.float32) ** shard_levels(seeds[1], (VARIANTS,), ((0, 16),), -0.2, 0.2), 0.6, 1.4)
    residual = draw_residual(jax.random.fold_in(seeds[7], 71), 0)
    latent_old = bell_draw(seeds[3], (TRAITS, N_VAR, N_VAR * CAP), 0.5, 3.0, ((1, 16),), jnp.float32)
    group_weight = jnp.clip(jnp.exp(math.log(40.0) - 3.6888795 * jax.random.uniform(seeds[4], (GROUPS,), jnp.float32) ** shard_levels(seeds[4], (GROUPS,), ((0, 16),), -0.2, 0.2)), 1.0, 40.0)
    copy_source = with_ends(jax.random.randint(seeds[5], (N_VAR, N_VAR, CAP), 0, VAR_DEV), jax.random.fold_in(seeds[5], 1), 0, VAR_DEV - 1).astype(jnp.int32)
    copy_slot = draw_copy_slot(jax.random.fold_in(seeds[7], 71), 0)
    return {"genotype": genotype, "dosage_mean": dosage_mean, "residual": residual, "latent_old": latent_old, "group_weight": group_weight, "copy_source": copy_source, "copy_slot": copy_slot}


step_length = 0.25

def block_products(residual, genotype):
    blocks = genotype.reshape(N_PEOPLE, PEOPLE_DEV, VARIANTS)
    pieces = residual.reshape(TRAITS, N_PEOPLE, PEOPLE_DEV).transpose(1, 0, 2)

    def one_block(carry, inputs):
        rows, dosage_block = inputs
        return (carry + jnp.dot(rows, dosage_block.astype(jnp.float32), precision=lax.Precision.HIGHEST), None)
    result, ignored = lax.scan(one_block, jnp.zeros((TRAITS, VARIANTS), jnp.float32), (pieces, blocks))
    return result

def block_predictions(coef_change, genotype):
    blocks = genotype.reshape(N_PEOPLE, PEOPLE_DEV, VARIANTS)

    def one_block(dosage_block):
        return lax.dot_general(coef_change, dosage_block.astype(jnp.float32), (((1,), (1,)), ((), ())), precision=lax.Precision.HIGHEST)
    outputs = lax.map(one_block, blocks)
    return outputs.transpose(1, 0, 2).reshape(TRAITS, N_PEOPLE * PEOPLE_DEV)

def reference(genotype, dosage_mean, residual, latent_old, group_weight, copy_source, copy_slot):
    inverse_root = 1.0 / math.sqrt(PEOPLE)
    list_length = N_VAR * CAP
    products = block_products(residual, genotype)
    residual_sums = lax.optimization_barrier(jnp.sum(residual, axis=1))
    correlation = (products - residual_sums[:, None] * dosage_mean[None, :]) * inverse_root
    global_ids = (jnp.arange(N_VAR, dtype=jnp.int32)[None, :, None] * VAR_DEV + copy_source).reshape(N_VAR, list_length)
    live_list = (copy_slot >= 0).reshape(N_VAR, list_length)
    owners = jnp.arange(N_VAR, dtype=jnp.int32)[:, None, None]
    group_ids = jnp.where(copy_slot >= 0, owners * GRP_DEV + copy_slot // GSIZE, GROUPS).reshape(N_VAR, list_length).astype(jnp.int32)
    live_float = live_list.astype(jnp.float32)
    picked = correlation[:, global_ids]
    grad_copy = picked * live_float[None]
    previous = latent_old * live_float[None]
    proposal = previous + step_length * grad_copy
    squares = lax.optimization_barrier(jnp.sum(proposal * proposal, axis=0))
    group_squares = jnp.zeros((GROUPS,), jnp.float32).at[group_ids.reshape(-1)].add(squares.reshape(-1), mode='drop')
    group_norm = jnp.sqrt(group_squares)
    threshold = step_length * group_weight
    shrinkage = jnp.maximum(group_norm - threshold, 0.0) / jnp.maximum(group_norm, threshold)
    safe = jnp.where(live_list, group_ids, 0).astype(jnp.int32)
    shrink_list = jnp.where(live_list, shrinkage[safe], 0.0)
    latent_new = proposal * shrink_list[None]
    changes = latent_new - previous
    coef_change = jnp.zeros((TRAITS, VARIANTS), jnp.float32).at[:, global_ids.reshape(-1)].add(changes.reshape(TRAITS, -1))
    predicted = block_predictions(coef_change, genotype)
    offset_term = jnp.dot(coef_change, dosage_mean, precision=lax.Precision.HIGHEST)
    residual_new = residual - (predicted - offset_term[:, None]) * inverse_root
    return (latent_new, coef_change, residual_new)
```

```python
import functools
import math

import jax
import jax.numpy as jnp
from jax import lax
from jax.experimental import pallas as pl
from jax.experimental.pallas import tpu as pltpu
from jax.sharding import PartitionSpec as P

MESH = pl.DeviceIdType.MESH
F32 = jnp.float32
BF16 = jnp.bfloat16
STEP = 0.25
LIST_ROWS = 56


def split3(a):
    first = a.astype(BF16).astype(F32)
    rest = a - first
    second = rest.astype(BF16).astype(F32)
    return first, second, rest - second


def kernel(n_people, n_var, inverse_root,
           geno, mean_h, res_h, lat_h, weight_h, source_h, slot_h,
           lat_out, coef_out, res_out,
           gi, gb, mean, res, lat, weight, source, slot,
           snd, rcv, pc, spc, zland, corr, tables, member, lows,
           prev, prop, squares, gland, thr, amat, latbuf, latland,
           cpart, csib, coef, pland, pbuf,
           in_sems, send_sems, recv_sems, out_sems):
    p, v = lax.axis_index("people"), lax.axis_index("var")
    n_z = n_people // 2
    core = lax.rem(p, 2)
    z = p // 2
    half = n_var // 2
    active = (v // half) == core
    sibling = {"people": p + 1 - 2 * core, "var": v}
    z_order = sorted(range(1, n_z), key=lambda d: -min(d, n_z - d))
    z_peers = [{"people": lax.rem(p + 2 * d, n_people), "var": v} for d in z_order]
    var_peers = [{"people": p, "var": lax.rem(v + d, n_var)} for d in range(1, n_var)]

    def local(src, dst, sem):
        copy = pltpu.make_async_copy(src, dst, sem)
        copy.start()
        return copy

    def remote(src, dst, k, device):
        copy = pltpu.make_async_remote_copy(src_ref=src, dst_ref=dst, send_sem=send_sems.at[k], recv_sem=recv_sems.at[k],
                                            device_id=device, device_id_type=MESH)
        copy.start()

    def drain(ref, sem):
        pltpu.make_async_copy(ref, ref, sem).wait()

    barrier = pltpu.get_barrier_semaphore()
    for device in z_peers + var_peers + [sibling]:
        pl.semaphore_signal(barrier, inc=1, device_id=device, device_id_type=MESH)

    people_dev = gi.shape[0]
    chunk = people_dev // 4
    small = [local(res_h, res, in_sems.at[4]), local(mean_h, mean, in_sems.at[5])]
    big = [local(geno.at[pl.ds(chunk * k, chunk), :], gi.at[pl.ds(chunk * k, chunk), :], in_sems.at[k]) for k in range(4)]
    lists = [local(lat_h, lat, in_sems.at[6]), local(weight_h, weight, in_sems.at[7]),
             local(source_h, source, in_sems.at[8]), local(slot_h, slot, in_sems.at[9])]

    for copy in small:
        copy.wait()
    residual = res[...]
    sums = jnp.sum(residual, axis=1, keepdims=True)
    parts = jnp.concatenate(split3(residual), axis=0).astype(BF16)
    total = None
    for k in range(4):
        big[k].wait()
        rows = pl.ds(chunk * k, chunk)
        block = gi[rows, :].astype(F32).astype(BF16)
        gb[rows, :] = block
        term = jnp.dot(parts[:, chunk * k:chunk * (k + 1)], block, preferred_element_type=F32)
        total = term if total is None else total + term
    products = total[8:12] + total[4:8] + total[0:4] - sums * mean[...]
    for h in range(8):
        pc[pl.ds(h, 4, stride=8), :] = products[:, 128 * h:128 * (h + 1)]

    for copy in lists:
        copy.wait()
    for i in range(n_var // 8):
        for j in range(8):
            block = pl.ds(8 * i * LIST_ROWS + 32 + j, 8, stride=LIST_ROWS)
            snd[block, :] = source[8 * i:8 * i + 8, 128 * j:128 * (j + 1)].astype(F32)
            block = pl.ds(8 * i * LIST_ROWS + 40 + j, 8, stride=LIST_ROWS)
            snd[block, :] = slot[8 * i:8 * i + 8, 128 * j:128 * (j + 1)].astype(F32)
    for s in range(n_var):
        for t in range(4):
            snd[LIST_ROWS * s + 8 * t:LIST_ROWS * s + 8 * t + 8, :] = lat[t, 8 * s:8 * s + 8, :]
        snd[LIST_ROWS * s + 48:LIST_ROWS * s + 56, :] = jnp.broadcast_to(weight[...], (8, 128))

    pl.semaphore_wait(barrier, n_z - 1 + n_var - 1 + 1)

    remote(pc, spc, 0, sibling)
    drain(pc, recv_sems.at[0])
    zland[z] = pc[...] + spc[...]
    for device in z_peers:
        remote(zland.at[z], zland.at[z], 1, device)

    def slab_rows(s):
        return pl.ds(pl.multiple_of(s * LIST_ROWS, 8), LIST_ROWS)

    mine = lax.rem(v, half)

    @pl.when(active)
    def _():
        for d in range(1, n_var):
            other = lax.rem(v + d, n_var)
            remote(snd.at[slab_rows(other), :], rcv.at[mine], 2, {"people": p, "var": other})
        rcv[mine] = snd[slab_rows(v), :]
        drain(rcv.at[pl.ds(0, half - 1)], recv_sems.at[2])

    @pl.when(jnp.logical_not(active))
    def _():
        drain(rcv, recv_sems.at[2])

    rows_iota = lax.broadcasted_iota(jnp.int32, (128, 128), 0)

    def prepare(o, carry):
        sources = rcv[o, 32:40, :].astype(jnp.int32)
        slots = rcv[o, 40:48, :].astype(jnp.int32)
        live = slots >= 0
        group = jnp.where(live, lax.shift_right_arithmetic(slots, 7), -1)
        low = lax.bitwise_and(sources, 127)
        for j in range(8):
            member[o, :, 128 * j:128 * (j + 1)] = jnp.where(rows_iota == group[j:j + 1, :], 1.0, 0.0).astype(BF16)
            lows[o, :, 128 * j:128 * (j + 1)] = jnp.where(rows_iota == low[j:j + 1, :], 1.0, 0.0).astype(BF16)
        for t in range(4):
            prev[o, 8 * t:8 * t + 8, :] = jnp.where(live, rcv[o, 8 * t:8 * t + 8, :], 0.0)
        thr[pl.ds(o, 1), :] = STEP * rcv[o, 48:49, :]
        return carry

    lax.fori_loop(0, half, prepare, 0)

    drain(zland.at[pl.ds(0, n_z - 1)], recv_sems.at[1])
    summed = zland[0]
    for k in range(1, n_z):
        summed = summed + zland[k]
    corr[...] = summed * inverse_root
    for t in range(4):
        for h in range(8):
            tables[8 * t + h] = jnp.broadcast_to(corr[8 * t + h:8 * t + h + 1, :], (8, 128))

    def propose(o, carry):
        sources = rcv[o, 32:40, :].astype(jnp.int32)
        live = rcv[o, 40:48, :] >= 0.0
        high = lax.shift_right_arithmetic(sources, 7)
        low = lax.bitwise_and(sources, 127)
        total = jnp.zeros((8, 128), F32)
        for t in range(4):
            picked = jnp.zeros((8, 128), F32)
            for h in range(8):
                picked = jnp.where(high == h, jnp.take_along_axis(tables[8 * t + h], low, axis=1), picked)
            value = prev[o, 8 * t:8 * t + 8, :] + STEP * jnp.where(live, picked, 0.0)
            prop[o, 8 * t:8 * t + 8, :] = value
            total = total + value * value
        squares[pl.ds(pl.multiple_of(8 * o, 8), 8), :] = total
        return carry

    lax.fori_loop(0, half, propose, 0)
    by_owner = jnp.concatenate([squares[pl.ds(j, half, stride=8), :] for j in range(8)], axis=1)
    stacked = jnp.concatenate(split3(by_owner), axis=0).astype(BF16)
    owner_iota = lax.broadcasted_iota(jnp.int32, (half, 128), 0)
    partial = jnp.zeros((half, 128), F32)
    for o in range(half):
        one = lax.dot_general(stacked, member[o], (((1,), (1,)), ((), ())), preferred_element_type=F32)
        one = one[2 * half:3 * half] + one[half:2 * half] + one[0:half]
        partial = jnp.where(owner_iota == o, one, partial)
    gland[v] = partial
    for device in var_peers:
        remote(gland.at[v], gland.at[v], 3, device)
    drain(gland.at[pl.ds(0, n_var - 1)], recv_sems.at[3])
    norm = gland[0]
    for k in range(1, n_var):
        norm = norm + gland[k]
    norm = jnp.sqrt(norm)
    threshold = thr[...]
    shrink = jnp.maximum(norm - threshold, 0.0) / jnp.maximum(norm, threshold)
    squares[0:half, :] = shrink

    hi_iota = lax.broadcasted_iota(jnp.int32, (8, 128), 0)

    def change(o, carry):
        slots = rcv[o, 40:48, :].astype(jnp.int32)
        live = slots >= 0
        group = jnp.where(live, lax.shift_right_arithmetic(slots, 7), 0)
        high = lax.shift_right_arithmetic(rcv[o, 32:40, :].astype(jnp.int32), 7)
        table = jnp.broadcast_to(squares[pl.ds(o, 1), :], (8, 128))
        factor = jnp.where(live, jnp.take_along_axis(table, group, axis=1), 0.0)
        deltas = []
        for t in range(4):
            fresh = prop[o, 8 * t:8 * t + 8, :] * factor
            latbuf[o, t] = fresh
            deltas.append(fresh - prev[o, 8 * t:8 * t + 8, :])
        for j in range(8):
            mask = hi_iota == high[j:j + 1, :]
            block = jnp.concatenate([jnp.where(mask, deltas[t][j:j + 1, :], 0.0) for t in range(4)], axis=0)
            first = block.astype(BF16)
            second = (block - first.astype(F32)).astype(BF16)
            amat[o, 0:32, 128 * j:128 * (j + 1)] = first
            amat[o, 32:64, 128 * j:128 * (j + 1)] = second
        return carry

    lax.fori_loop(0, half, change, 0)
    acc = jnp.zeros((64, 128), F32)
    for o in range(half):
        acc = acc + lax.dot_general(amat[o], lows[o], (((1,), (1,)), ((), ())), preferred_element_type=F32)
    cpart[...] = acc[32:64] + acc[0:32]
    remote(cpart, csib, 4, sibling)

    slab_place = pl.ds(pl.multiple_of(8 * v, 8), 8)
    for o in range(half):
        owner = core * half + o

        @pl.when(owner != v)
        def _():
            remote(latbuf.at[o], latland.at[:, slab_place, :], 5, {"people": p, "var": owner})

    @pl.when(active)
    def _():
        latland[:, slab_place, :] = latbuf[mine]

    drain(cpart, recv_sems.at[4])
    coef[...] = cpart[...] + csib[...]
    wide = jnp.concatenate([coef[pl.ds(h, 4, stride=8), :] for h in range(8)], axis=1)
    coef_out[...] = wide
    offset = jnp.sum(wide * mean[...], axis=1, keepdims=True)
    pieces = jnp.concatenate(split3(wide), axis=0).astype(BF16)
    fitted = lax.dot_general(pieces, gb[...], (((1,), (1,)), ((), ())), preferred_element_type=F32)
    fitted = fitted[8:12] + fitted[4:8] + fitted[0:4] - offset
    lanes = people_dev // 128
    for k in range(lanes):
        pbuf[4 * k:4 * k + 4, :] = fitted[:, 128 * k:128 * (k + 1)]
    pland[v] = pbuf[...]
    for device in var_peers:
        remote(pland.at[v], pland.at[v], 6, device)

    @pl.when(active)
    def _():
        drain(latland.at[:, pl.ds(0, 8 * (n_var - 1)), :], recv_sems.at[5])
        remote(latland, latland, 7, sibling)

    @pl.when(jnp.logical_not(active))
    def _():
        drain(latland, recv_sems.at[7])

    local(latland, lat_out, out_sems.at[0])

    drain(pland.at[pl.ds(0, n_var - 1)], recv_sems.at[6])
    predicted = pland[0]
    for k in range(1, n_var):
        predicted = predicted + pland[k]
    for k in range(lanes):
        res_out[:, 128 * k:128 * (k + 1)] = residual[:, 128 * k:128 * (k + 1)] - predicted[4 * k:4 * k + 4, :] * inverse_root

    drain(lat_out, out_sems.at[0])
    drain(pc, send_sems.at[0])
    drain(zland.at[pl.ds(0, n_z - 1)], send_sems.at[1])
    drain(gland.at[pl.ds(0, n_var - 1)], send_sems.at[3])
    drain(cpart, send_sems.at[4])
    drain(pland.at[pl.ds(0, n_var - 1)], send_sems.at[6])

    @pl.when(active)
    def _():
        drain(snd.at[pl.ds(0, LIST_ROWS * (n_var - 1)), :], send_sems.at[2])
        drain(latbuf.at[pl.ds(0, half - 1)], send_sems.at[5])
        drain(latland, send_sems.at[7])

    @pl.when(jnp.logical_not(active))
    def _():
        drain(latbuf, send_sems.at[5])


def per_device(n_people, n_var, genotype, dosage_mean, residual, latent_old, group_weight, copy_source, copy_slot):
    people_dev, var_dev = genotype.shape
    traits = residual.shape[0]
    inverse_root = 1.0 / math.sqrt(people_dev * n_people)
    half = n_var // 2
    n_z = n_people // 2
    list_rows = n_var * var_dev // 128
    vmem = pl.BlockSpec(memory_space=pltpu.VMEM)
    hbm = pl.BlockSpec(memory_space=pl.ANY)
    lat, coef, res = pl.pallas_call(
        functools.partial(kernel, n_people, n_var, inverse_root),
        out_shape=(
            jax.ShapeDtypeStruct((traits, list_rows, 128), F32),
            jax.ShapeDtypeStruct((traits, var_dev), F32),
            jax.ShapeDtypeStruct((traits, people_dev), F32),
        ),
        in_specs=[hbm] * 7,
        out_specs=(hbm, vmem, vmem),
        scratch_shapes=[
            pltpu.VMEM((people_dev, var_dev), jnp.int32),
            pltpu.VMEM((people_dev, var_dev), BF16),
            pltpu.VMEM((1, var_dev), F32),
            pltpu.VMEM((traits, people_dev), F32),
            pltpu.VMEM((traits, list_rows, 128), F32),
            pltpu.VMEM((1, 128), F32),
            pltpu.VMEM((n_var, 1024), jnp.int32),
            pltpu.VMEM((n_var, 1024), jnp.int32),
            pltpu.VMEM((n_var * LIST_ROWS, 128), F32),
            pltpu.VMEM((half, LIST_ROWS, 128), F32),
            pltpu.VMEM((32, 128), F32),
            pltpu.VMEM((32, 128), F32),
            pltpu.VMEM((n_z, 32, 128), F32),
            pltpu.VMEM((32, 128), F32),
            pltpu.VMEM((32, 8, 128), F32),
            pltpu.VMEM((half, 128, 1024), BF16),
            pltpu.VMEM((half, 128, 1024), BF16),
            pltpu.VMEM((half, 32, 128), F32),
            pltpu.VMEM((half, 32, 128), F32),
            pltpu.VMEM((half * 8, 128), F32),
            pltpu.VMEM((n_var, half, 128), F32),
            pltpu.VMEM((half, 128), F32),
            pltpu.VMEM((half, 64, 1024), BF16),
            pltpu.VMEM((half, traits, 8, 128), F32),
            pltpu.VMEM((traits, list_rows, 128), F32),
            pltpu.VMEM((32, 128), F32),
            pltpu.VMEM((32, 128), F32),
            pltpu.VMEM((32, 128), F32),
            pltpu.VMEM((n_var, people_dev // 32, 128), F32),
            pltpu.VMEM((people_dev // 32, 128), F32),
            pltpu.SemaphoreType.DMA((10,)),
            pltpu.SemaphoreType.DMA((8,)),
            pltpu.SemaphoreType.DMA((8,)),
            pltpu.SemaphoreType.DMA((1,)),
        ],
        compiler_params=pltpu.CompilerParams(collective_id=0, has_side_effects=True, vmem_limit_bytes=62 * 2**20),
    )(
        genotype,
        dosage_mean.reshape(1, var_dev),
        residual,
        latent_old.reshape(traits, list_rows, 128),
        group_weight.reshape(1, 128),
        copy_source[0],
        copy_slot[0],
    )
    return lat.reshape(latent_old.shape), coef, res


def solution(mesh):
    return jax.shard_map(
        functools.partial(per_device, mesh.shape["people"], mesh.shape["var"]),
        mesh=mesh,
        in_specs=(
            P("people", "var"),
            P("var"),
            P(None, "people"),
            P(None, "var", None),
            P("var"),
            P("var", None, None),
            P("var", None, None),
        ),
        out_specs=(P(None, "var", None), P(None, "var"), P(None, "people")),
        check_vma=False,
    )
```

```python
import functools
import math

import jax
import jax.numpy as jnp
from jax import lax
from jax.experimental import pallas as pl
from jax.experimental.pallas import tpu as pltpu
from jax.sharding import PartitionSpec as P

MESH = pl.DeviceIdType.MESH
F32 = jnp.float32
BF16 = jnp.bfloat16
STEP = 0.25
LIST_ROWS = 56


def split3(a):
    first = a.astype(BF16).astype(F32)
    rest = a - first
    second = rest.astype(BF16).astype(F32)
    return first, second, rest - second


def kernel(n_people, n_var, inverse_root,
           geno, mean_h, res_h, lat_h, weight_h, source_h, slot_h,
           lat_out, coef_out, res_out,
           gi, gb, mean, res, lat, weight, source, slot,
           snd, rcv, pc, win, wsum, halves, corr, tables, member, lows,
           highs, prev, prop, squares, gland, thr, amat, latbuf, latland,
           cpart, csib, coef, pland, pbuf,
           in_sems, send_sems, recv_sems):
    p, v = lax.axis_index("people"), lax.axis_index("var")
    n_z = n_people // 2
    core = lax.rem(p, 2)
    z = p // 2
    half = n_var // 2
    active = (v // half) == core
    sibling = {"people": p + 1 - 2 * core, "var": v}
    reach = n_z // 4

    def along(d, other=False):
        return {"people": 2 * lax.rem(z + d + n_z, n_z) + (1 - core if other else core), "var": v}

    near = sorted((d for d in range(-reach, reach + 1) if d != 0), key=lambda d: -abs(d))
    z_peers = [along(d) for d in near] + [along(reach, True), along(-reach, True)]
    var_peers = [{"people": p, "var": lax.rem(v + d, n_var)} for d in range(1, n_var)]

    def local(src, dst, sem):
        copy = pltpu.make_async_copy(src, dst, sem)
        copy.start()
        return copy

    def remote(src, dst, k, device):
        copy = pltpu.make_async_remote_copy(src_ref=src, dst_ref=dst, send_sem=send_sems.at[k], recv_sem=recv_sems.at[k],
                                            device_id=device, device_id_type=MESH)
        copy.start()

    def drain(ref, sem):
        pltpu.make_async_copy(ref, ref, sem).wait()

    barrier = pltpu.get_barrier_semaphore()
    for device in z_peers + var_peers + [sibling]:
        pl.semaphore_signal(barrier, inc=1, device_id=device, device_id_type=MESH)

    people_dev = gi.shape[0]
    chunk = people_dev // 4
    small = [local(res_h, res, in_sems.at[4]), local(mean_h, mean, in_sems.at[5])]
    big = [local(geno.at[pl.ds(chunk * k, chunk), :], gi.at[pl.ds(chunk * k, chunk), :], in_sems.at[k]) for k in range(4)]
    lists = [local(lat_h, lat, in_sems.at[6]), local(weight_h, weight, in_sems.at[7]),
             local(source_h, source, in_sems.at[8]), local(slot_h, slot, in_sems.at[9])]

    for copy in small:
        copy.wait()
    residual = res[...]
    sums = jnp.sum(residual, axis=1, keepdims=True)
    parts = jnp.concatenate(split3(residual), axis=0).astype(BF16)
    total = None
    for k in range(4):
        big[k].wait()
        rows = pl.ds(chunk * k, chunk)
        block = gi[rows, :].astype(F32).astype(BF16)
        gb[rows, :] = block
        term = jnp.dot(parts[:, chunk * k:chunk * (k + 1)], block, preferred_element_type=F32)
        total = term if total is None else total + term
    products = total[8:12] + total[4:8] + total[0:4] - sums * mean[...]
    for h in range(8):
        pc[pl.ds(h, 4, stride=8), :] = products[:, 128 * h:128 * (h + 1)]

    for copy in lists:
        copy.wait()
    for i in range(n_var // 8):
        for j in range(8):
            block = pl.ds(8 * i * LIST_ROWS + 32 + j, 8, stride=LIST_ROWS)
            snd[block, :] = source[8 * i:8 * i + 8, 128 * j:128 * (j + 1)].astype(F32)
            block = pl.ds(8 * i * LIST_ROWS + 40 + j, 8, stride=LIST_ROWS)
            snd[block, :] = slot[8 * i:8 * i + 8, 128 * j:128 * (j + 1)].astype(F32)
    for s in range(n_var):
        for t in range(4):
            snd[LIST_ROWS * s + 8 * t:LIST_ROWS * s + 8 * t + 8, :] = lat[t, 8 * s:8 * s + 8, :]
        snd[LIST_ROWS * s + 48:LIST_ROWS * s + 56, :] = jnp.broadcast_to(weight[...], (8, 128))

    pl.semaphore_wait(barrier, len(z_peers) + len(var_peers) + 1)

    win[reach] = pc[...]
    for d in near:
        if d < reach:
            remote(pc, win.at[reach + d], 1, along(-d))

    def slab_rows(s):
        return pl.ds(pl.multiple_of(s * LIST_ROWS, 8), LIST_ROWS)

    mine = lax.rem(v, half)

    @pl.when(active)
    def _():
        for d in range(1, n_var):
            other = lax.rem(v + d, n_var)
            remote(snd.at[slab_rows(other), :], rcv.at[mine], 2, {"people": p, "var": other})
        rcv[mine] = snd[slab_rows(v), :]

    drain(win.at[pl.ds(0, 2 * reach - 1)], recv_sems.at[1])
    summed = win[0]
    for k in range(1, 2 * reach):
        summed = summed + win[k]
    wsum[...] = summed
    for k, d in enumerate((-reach, reach)):
        for other in (False, True):
            remote(wsum, halves.at[2 * core + k], 0, along(d, other))

    @pl.when(active)
    def _():
        drain(rcv.at[pl.ds(0, half - 1)], recv_sems.at[2])

    @pl.when(jnp.logical_not(active))
    def _():
        drain(rcv, recv_sems.at[2])

    rows_iota = lax.broadcasted_iota(jnp.int32, (128, 128), 0)
    lanes_iota = lax.broadcasted_iota(jnp.int32, (128, 128), 1)
    hi_iota = lax.broadcasted_iota(jnp.int32, (8, 128), 0)

    def prepare(o, carry):
        sources = rcv[o, 32:40, :].astype(jnp.int32)
        slots = rcv[o, 40:48, :].astype(jnp.int32)
        live = slots >= 0
        group = jnp.where(live, lax.shift_right_arithmetic(slots, 7), -1)
        low = lax.bitwise_and(sources, 127)
        high = lax.shift_right_arithmetic(sources, 7)
        low_columns = low.T
        for j in range(8):
            rows = pl.ds(pl.multiple_of(128 * o, 128), 128)
            member[rows, 128 * j:128 * (j + 1)] = jnp.where(rows_iota == group[j:j + 1, :], 1.0, 0.0).astype(BF16)
            rows = pl.ds(pl.multiple_of(1024 * o + 128 * j, 128), 128)
            lows[rows, :] = jnp.where(lanes_iota == low_columns[:, j:j + 1], 1.0, 0.0).astype(BF16)
            highs[8 * o + j] = jnp.where(hi_iota == high[j:j + 1, :], 1.0, 0.0)
        for t in range(4):
            prev[o, 8 * t:8 * t + 8, :] = jnp.where(live, rcv[o, 8 * t:8 * t + 8, :], 0.0)
        thr[pl.ds(o, 1), :] = STEP * rcv[o, 48:49, :]
        return carry

    lax.fori_loop(0, half, prepare, 0)

    drain(halves, recv_sems.at[0])
    corr[...] = ((halves[0] + halves[1]) + (halves[2] + halves[3])) * inverse_root
    for t in range(4):
        for h in range(8):
            tables[8 * t + h] = jnp.broadcast_to(corr[8 * t + h:8 * t + h + 1, :], (8, 128))

    for o in range(half):
        sources = rcv[o, 32:40, :].astype(jnp.int32)
        live = rcv[o, 40:48, :] >= 0.0
        high = lax.shift_right_arithmetic(sources, 7)
        low = lax.bitwise_and(sources, 127)
        total = jnp.zeros((8, 128), F32)
        for t in range(4):
            picked = jnp.zeros((8, 128), F32)
            for h in range(8):
                picked = jnp.where(high == h, jnp.take_along_axis(tables[8 * t + h], low, axis=1), picked)
            value = prev[o, 8 * t:8 * t + 8, :] + STEP * jnp.where(live, picked, 0.0)
            prop[o, 8 * t:8 * t + 8, :] = value
            total = total + value * value
        squares[8 * o:8 * o + 8, :] = total
    by_owner = jnp.concatenate([squares[pl.ds(j, half, stride=8), :] for j in range(8)], axis=1)
    stacked = jnp.concatenate(split3(by_owner), axis=0).astype(BF16)
    owner_iota = lax.broadcasted_iota(jnp.int32, (half, 128), 0)
    wide = lax.dot_general(stacked, member[...], (((1,), (1,)), ((), ())), preferred_element_type=F32)
    wide = wide[2 * half:3 * half] + wide[half:2 * half] + wide[0:half]
    partial = wide[:, 0:128]
    for o in range(1, half):
        partial = jnp.where(owner_iota == o, wide[:, 128 * o:128 * (o + 1)], partial)
    gland[v] = partial
    for device in var_peers:
        remote(gland.at[v], gland.at[v], 3, device)
    drain(gland.at[pl.ds(0, n_var - 1)], recv_sems.at[3])
    norm = gland[0]
    for k in range(1, n_var):
        norm = norm + gland[k]
    norm = jnp.sqrt(norm)
    threshold = thr[...]
    shrink = jnp.maximum(norm - threshold, 0.0) / jnp.maximum(norm, threshold)
    squares[0:half, :] = shrink

    slab_place = pl.ds(pl.multiple_of(8 * v, 8), 8)
    for o in range(half):
        slots = rcv[o, 40:48, :].astype(jnp.int32)
        live = slots >= 0
        group = jnp.where(live, lax.shift_right_arithmetic(slots, 7), 0)
        table = jnp.broadcast_to(squares[o:o + 1, :], (8, 128))
        factor = jnp.where(live, jnp.take_along_axis(table, group, axis=1), 0.0)
        firsts, seconds = [], []
        for t in range(4):
            fresh = prop[o, 8 * t:8 * t + 8, :] * factor
            latbuf[o, t] = fresh
            delta = fresh - prev[o, 8 * t:8 * t + 8, :]
            first = delta.astype(BF16).astype(F32)
            firsts.append(first)
            seconds.append(delta - first)
        for j in range(8):
            mask = highs[8 * o + j]
            for k, terms in enumerate((firsts, seconds)):
                block = jnp.concatenate([mask * term[j:j + 1, :] for term in terms], axis=0)
                amat[32 * k:32 * k + 32, 1024 * o + 128 * j:1024 * o + 128 * (j + 1)] = block.astype(BF16)

    for o in range(half):
        owner = core * half + o

        @pl.when(owner != v)
        def _():
            remote(latbuf.at[o], latland.at[:, slab_place, :], 5, {"people": p, "var": owner})

    @pl.when(active)
    def _():
        latland[:, slab_place, :] = latbuf[mine]

    acc = jnp.dot(amat[...], lows[...], preferred_element_type=F32)
    cpart[...] = acc[32:64] + acc[0:32]
    remote(cpart, csib, 4, sibling)

    drain(cpart, recv_sems.at[4])
    coef[...] = cpart[...] + csib[...]
    wide = jnp.concatenate([coef[pl.ds(h, 4, stride=8), :] for h in range(8)], axis=1)
    coef_out[...] = wide
    offset = jnp.sum(wide * mean[...], axis=1, keepdims=True)
    pieces = jnp.concatenate(split3(wide), axis=0).astype(BF16)
    fitted = lax.dot_general(pieces, gb[...], (((1,), (1,)), ((), ())), preferred_element_type=F32)
    fitted = fitted[8:12] + fitted[4:8] + fitted[0:4] - offset
    lanes = people_dev // 128
    for k in range(lanes):
        pbuf[4 * k:4 * k + 4, :] = fitted[:, 128 * k:128 * (k + 1)]
    pland[v] = pbuf[...]
    for device in var_peers:
        remote(pland.at[v], pland.at[v], 6, device)

    @pl.when(active)
    def _():
        drain(latland.at[:, pl.ds(0, 8 * (n_var - 1)), :], recv_sems.at[5])
        remote(latland, latland, 7, sibling)

    @pl.when(jnp.logical_not(active))
    def _():
        drain(latland, recv_sems.at[7])

    lat_out[...] = latland[...]

    drain(pland.at[pl.ds(0, n_var - 1)], recv_sems.at[6])
    predicted = pland[0]
    for k in range(1, n_var):
        predicted = predicted + pland[k]
    for k in range(lanes):
        res_out[:, 128 * k:128 * (k + 1)] = residual[:, 128 * k:128 * (k + 1)] - predicted[4 * k:4 * k + 4, :] * inverse_root

    drain(halves, send_sems.at[0])
    drain(win.at[pl.ds(0, 2 * reach - 1)], send_sems.at[1])
    drain(gland.at[pl.ds(0, n_var - 1)], send_sems.at[3])
    drain(cpart, send_sems.at[4])
    drain(pland.at[pl.ds(0, n_var - 1)], send_sems.at[6])

    @pl.when(active)
    def _():
        drain(snd.at[pl.ds(0, LIST_ROWS * (n_var - 1)), :], send_sems.at[2])
        drain(latbuf.at[pl.ds(0, half - 1)], send_sems.at[5])
        drain(latland, send_sems.at[7])

    @pl.when(jnp.logical_not(active))
    def _():
        drain(latbuf, send_sems.at[5])


def hand_out(lat, coef, res, lat_out, coef_out, res_out, sems):
    copies = [pltpu.make_async_copy(src, dst, sems.at[k])
              for k, (src, dst) in enumerate(((lat, lat_out), (coef, coef_out), (res, res_out)))]
    for copy in copies:
        copy.start()
    for copy in copies:
        copy.wait()


def per_device(n_people, n_var, genotype, dosage_mean, residual, latent_old, group_weight, copy_source, copy_slot):
    people_dev, var_dev = genotype.shape
    traits = residual.shape[0]
    inverse_root = 1.0 / math.sqrt(people_dev * n_people)
    half = n_var // 2
    n_z = n_people // 2
    list_rows = n_var * var_dev // 128
    vmem = pl.BlockSpec(memory_space=pltpu.VMEM)
    hbm = pl.BlockSpec(memory_space=pltpu.HBM)
    shapes = ((traits, list_rows, 128), (traits, var_dev), (traits, people_dev))
    held = pl.pallas_call(
        functools.partial(kernel, n_people, n_var, inverse_root),
        out_shape=tuple(pltpu.VMEM(shape, F32) for shape in shapes),
        in_specs=[hbm] * 7,
        out_specs=(vmem,) * 3,
        scratch_shapes=[
            pltpu.VMEM((people_dev, var_dev), jnp.int32),
            pltpu.VMEM((people_dev, var_dev), BF16),
            pltpu.VMEM((1, var_dev), F32),
            pltpu.VMEM((traits, people_dev), F32),
            pltpu.VMEM((traits, list_rows, 128), F32),
            pltpu.VMEM((1, 128), F32),
            pltpu.VMEM((n_var, 1024), jnp.int32),
            pltpu.VMEM((n_var, 1024), jnp.int32),
            pltpu.VMEM((n_var * LIST_ROWS, 128), F32),
            pltpu.VMEM((half, LIST_ROWS, 128), F32),
            pltpu.VMEM((32, 128), F32),
            pltpu.VMEM((n_z // 2, 32, 128), F32),
            pltpu.VMEM((32, 128), F32),
            pltpu.VMEM((4, 32, 128), F32),
            pltpu.VMEM((32, 128), F32),
            pltpu.VMEM((32, 8, 128), F32),
            pltpu.VMEM((half * 128, 1024), BF16),
            pltpu.VMEM((half * 1024, 128), BF16),
            pltpu.VMEM((half * 8, 8, 128), F32),
            pltpu.VMEM((half, 32, 128), F32),
            pltpu.VMEM((half, 32, 128), F32),
            pltpu.VMEM((half * 8, 128), F32),
            pltpu.VMEM((n_var, half, 128), F32),
            pltpu.VMEM((half, 128), F32),
            pltpu.VMEM((64, half * 1024), BF16),
            pltpu.VMEM((half, traits, 8, 128), F32),
            pltpu.VMEM((traits, list_rows, 128), F32),
            pltpu.VMEM((32, 128), F32),
            pltpu.VMEM((32, 128), F32),
            pltpu.VMEM((32, 128), F32),
            pltpu.VMEM((n_var, people_dev // 32, 128), F32),
            pltpu.VMEM((people_dev // 32, 128), F32),
            pltpu.SemaphoreType.DMA((10,)),
            pltpu.SemaphoreType.DMA((8,)),
            pltpu.SemaphoreType.DMA((8,)),
        ],
        compiler_params=pltpu.CompilerParams(collective_id=0, has_side_effects=True, vmem_limit_bytes=32 * 2**20),
    )(*(pltpu.with_memory_space_constraint(x, pltpu.HBM) for x in (
        genotype,
        dosage_mean.reshape(1, var_dev),
        residual,
        latent_old.reshape(traits, list_rows, 128),
        group_weight.reshape(1, 128),
        copy_source[0],
        copy_slot[0],
    )))
    lat, coef, res = pl.pallas_call(
        hand_out,
        out_shape=tuple(jax.ShapeDtypeStruct(shape, F32) for shape in shapes),
        in_specs=[vmem] * 3,
        out_specs=(hbm,) * 3,
        scratch_shapes=[pltpu.SemaphoreType.DMA((3,))],
    )(*(pltpu.with_memory_space_constraint(x, pltpu.VMEM) for x in held))
    return lat.reshape(latent_old.shape), coef, res


def solution(mesh):
    return jax.shard_map(
        functools.partial(per_device, mesh.shape["people"], mesh.shape["var"]),
        mesh=mesh,
        in_specs=(
            P("people", "var"),
            P("var"),
            P(None, "people"),
            P(None, "var", None),
            P("var"),
            P("var", None, None),
            P("var", None, None),
        ),
        out_specs=(P(None, "var", None), P(None, "var"), P(None, "people")),
        check_vma=False,
    )
```

```python
import functools
import math

import jax
import jax.numpy as jnp
from jax import lax
from jax.experimental import pallas as pl
from jax.experimental.pallas import tpu as pltpu
from jax.sharding import PartitionSpec as P

MESH = pl.DeviceIdType.MESH
F32 = jnp.float32
BF16 = jnp.bfloat16
STEP = 0.25
LIST_ROWS = 56


def split3(a):
    first = a.astype(BF16).astype(F32)
    rest = a - first
    second = rest.astype(BF16).astype(F32)
    return first, second, rest - second


def kernel(n_people, n_var, inverse_root,
           geno, mean_h, res_h, lat_h, weight_h, source_h, slot_h,
           lat_out, coef_out, res_out,
           gi, gb, mean, res, lat, weight, source, slot,
           snd, rcv, pc, win, wsum, halves, corr, tables, member, lows,
           highs, prev, prop, squares, gland, thr, amat, cland, own,
           cpart, csib, coef, pland, pbuf,
           in_sems, send_sems, recv_sems):
    p, v = lax.axis_index("people"), lax.axis_index("var")
    n_z = n_people // 2
    core = lax.rem(p, 2)
    z = p // 2
    half = n_var // 2
    active = (v // half) == core
    sibling = {"people": p + 1 - 2 * core, "var": v}
    reach = n_z // 4

    def along(d, on):
        return {"people": 2 * lax.rem(z + d + n_z, n_z) + on, "var": v}

    near = sorted((d for d in range(-reach, reach + 1) if d != 0), key=lambda d: -abs(d))
    z_peers = [along(d, on) for d in near for on in (0, 1)]
    side = math.isqrt(n_var)
    vy, vx = v // side, lax.rem(v, side)

    def in_plane(dy, dx):
        return {"people": p, "var": lax.rem(vy + dy, side) * side + lax.rem(vx + dx, side)}

    def hops(offset):
        return sum(min(d, side - d) for d in offset)

    offsets = [(dy, dx) for dy in range(side) for dx in range(side) if dy or dx]
    var_peers = [in_plane(dy, dx) for dy, dx in sorted(offsets, key=hops, reverse=True)]

    def local(src, dst, sem):
        copy = pltpu.make_async_copy(src, dst, sem)
        copy.start()
        return copy

    def remote(src, dst, k, device):
        copy = pltpu.make_async_remote_copy(src_ref=src, dst_ref=dst, send_sem=send_sems.at[k], recv_sem=recv_sems.at[k],
                                            device_id=device, device_id_type=MESH)
        copy.start()

    def drain(ref, sem):
        pltpu.make_async_copy(ref, ref, sem).wait()

    barrier = pltpu.get_barrier_semaphore()
    for device in z_peers + var_peers + [sibling]:
        pl.semaphore_signal(barrier, inc=1, device_id=device, device_id_type=MESH)

    people_dev = gi.shape[0]
    chunk = people_dev // 4
    small = [local(res_h, res, in_sems.at[4]), local(mean_h, mean, in_sems.at[5])]
    big = [local(geno.at[pl.ds(chunk * k, chunk), :], gi.at[pl.ds(chunk * k, chunk), :], in_sems.at[k]) for k in range(4)]
    lists = [local(lat_h, lat, in_sems.at[6]), local(weight_h, weight, in_sems.at[7]),
             local(source_h, source, in_sems.at[8]), local(slot_h, slot, in_sems.at[9])]

    for copy in small:
        copy.wait()
    residual = res[...]
    sums = jnp.sum(residual, axis=1, keepdims=True)
    parts = jnp.concatenate(split3(residual), axis=0).astype(BF16)
    total = None
    for k in range(4):
        big[k].wait()
        rows = pl.ds(chunk * k, chunk)
        block = gi[rows, :].astype(F32).astype(BF16)
        gb[rows, :] = block
        term = jnp.dot(parts[:, chunk * k:chunk * (k + 1)], block, preferred_element_type=F32)
        total = term if total is None else total + term
    products = total[8:12] + total[4:8] + total[0:4] - sums * mean[...]
    for h in range(8):
        pc[pl.ds(h, 4, stride=8), :] = products[:, 128 * h:128 * (h + 1)]

    for copy in lists:
        copy.wait()
    for i in range(n_var // 8):
        for j in range(8):
            block = pl.ds(8 * i * LIST_ROWS + 32 + j, 8, stride=LIST_ROWS)
            snd[block, :] = source[8 * i:8 * i + 8, 128 * j:128 * (j + 1)].astype(F32)
            block = pl.ds(8 * i * LIST_ROWS + 40 + j, 8, stride=LIST_ROWS)
            snd[block, :] = slot[8 * i:8 * i + 8, 128 * j:128 * (j + 1)].astype(F32)
    for s in range(n_var):
        for t in range(4):
            snd[LIST_ROWS * s + 8 * t:LIST_ROWS * s + 8 * t + 8, :] = lat[t, 8 * s:8 * s + 8, :]
        snd[LIST_ROWS * s + 48:LIST_ROWS * s + 56, :] = jnp.broadcast_to(weight[...], (8, 128))

    pl.semaphore_wait(barrier, len(z_peers) + len(var_peers) + 1)

    own_rows = pl.ds(pl.multiple_of(16 * core, 16), 16)
    other_rows = pl.ds(pl.multiple_of(16 - 16 * core, 16), 16)
    for d in near:
        if d < reach:
            for on in (0, 1):
                remote(pc.at[pl.ds(16 * on, 16), :], win.at[2 * (reach + d) + core], 1, along(-d, on))
    remote(pc.at[other_rows, :], win.at[2 * reach + core], 1, sibling)
    win[2 * reach + core] = pc[own_rows, :]

    def slab_rows(s):
        return pl.ds(pl.multiple_of(s * LIST_ROWS, 8), LIST_ROWS)

    mine = lax.rem(v, half)

    @pl.when(active)
    def _():
        for device in var_peers:
            remote(snd.at[slab_rows(device["var"]), :], rcv.at[mine], 2, device)
        rcv[mine] = snd[slab_rows(v), :]

    drain(win.at[pl.ds(0, 4 * reach - 1)], recv_sems.at[1])
    summed = win[0]
    for k in range(1, 4 * reach):
        summed = summed + win[k]
    wsum[...] = summed
    for k, d in enumerate((-reach, reach)):
        for on in (0, 1):
            remote(wsum, halves.at[k, own_rows, :], 0, along(d, on))

    @pl.when(active)
    def _():
        drain(rcv.at[pl.ds(0, half - 1)], recv_sems.at[2])

    @pl.when(jnp.logical_not(active))
    def _():
        drain(rcv, recv_sems.at[2])

    rows_iota = lax.broadcasted_iota(jnp.int32, (128, 128), 0)
    lanes_iota = lax.broadcasted_iota(jnp.int32, (128, 128), 1)
    hi_iota = lax.broadcasted_iota(jnp.int32, (8, 128), 0)

    def prepare(o, carry):
        sources = rcv[o, 32:40, :].astype(jnp.int32)
        slots = rcv[o, 40:48, :].astype(jnp.int32)
        live = slots >= 0
        group = jnp.where(live, lax.shift_right_arithmetic(slots, 7), -1)
        low = lax.bitwise_and(sources, 127)
        high = lax.shift_right_arithmetic(sources, 7)
        low_columns = low.T
        for j in range(8):
            rows = pl.ds(pl.multiple_of(128 * o, 128), 128)
            member[rows, 128 * j:128 * (j + 1)] = jnp.where(rows_iota == group[j:j + 1, :], 1.0, 0.0).astype(BF16)
            rows = pl.ds(pl.multiple_of(1024 * o + 128 * j, 128), 128)
            lows[rows, :] = jnp.where(lanes_iota == low_columns[:, j:j + 1], 1.0, 0.0).astype(BF16)
            highs[8 * o + j] = jnp.where(hi_iota == high[j:j + 1, :], 1.0, 0.0)
        for t in range(4):
            prev[o, 8 * t:8 * t + 8, :] = jnp.where(live, rcv[o, 8 * t:8 * t + 8, :], 0.0)
        thr[pl.ds(o, 1), :] = STEP * rcv[o, 48:49, :]
        return carry

    lax.fori_loop(0, half, prepare, 0)

    drain(halves, recv_sems.at[0])
    corr[...] = (halves[0] + halves[1]) * inverse_root
    for t in range(4):
        for h in range(8):
            tables[8 * t + h] = jnp.broadcast_to(corr[8 * t + h:8 * t + h + 1, :], (8, 128))

    for o in range(half):
        sources = rcv[o, 32:40, :].astype(jnp.int32)
        live = rcv[o, 40:48, :] >= 0.0
        high = lax.shift_right_arithmetic(sources, 7)
        low = lax.bitwise_and(sources, 127)
        total = jnp.zeros((8, 128), F32)
        for t in range(4):
            picked = jnp.zeros((8, 128), F32)
            for h in range(8):
                picked = jnp.where(high == h, jnp.take_along_axis(tables[8 * t + h], low, axis=1), picked)
            value = prev[o, 8 * t:8 * t + 8, :] + STEP * jnp.where(live, picked, 0.0)
            prop[o, 8 * t:8 * t + 8, :] = value
            total = total + value * value
        squares[8 * o:8 * o + 8, :] = total
    by_owner = jnp.concatenate([squares[pl.ds(j, half, stride=8), :] for j in range(8)], axis=1)
    stacked = jnp.concatenate(split3(by_owner), axis=0).astype(BF16)
    owner_iota = lax.broadcasted_iota(jnp.int32, (half, 128), 0)
    wide = lax.dot_general(stacked, member[...], (((1,), (1,)), ((), ())), preferred_element_type=F32)
    wide = wide[2 * half:3 * half] + wide[half:2 * half] + wide[0:half]
    partial = wide[:, 0:128]
    for o in range(1, half):
        partial = jnp.where(owner_iota == o, wide[:, 128 * o:128 * (o + 1)], partial)
    gland[v] = partial
    for device in var_peers:
        remote(gland.at[v], gland.at[v], 3, device)

    cland[v, own_rows, :] = corr[own_rows, :]
    for device in var_peers:
        remote(cland.at[v, own_rows, :], cland.at[v, own_rows, :], 5, device)
    drain(gland.at[pl.ds(0, n_var - 1)], recv_sems.at[3])
    norm = gland[0]
    for k in range(1, n_var):
        norm = norm + gland[k]
    norm = jnp.sqrt(norm)
    threshold = thr[...]
    shrink = jnp.maximum(norm - threshold, 0.0) / jnp.maximum(norm, threshold)
    squares[0:half, :] = shrink

    @pl.when(active)
    def _():
        own[...] = squares[pl.ds(mine, 1), :]
        remote(own, own, 7, sibling)

    acc = None
    for o in range(half):
        slots = rcv[o, 40:48, :].astype(jnp.int32)
        live = slots >= 0
        group = jnp.where(live, lax.shift_right_arithmetic(slots, 7), 0)
        table = jnp.broadcast_to(squares[o:o + 1, :], (8, 128))
        factor = jnp.where(live, jnp.take_along_axis(table, group, axis=1), 0.0)
        firsts, seconds = [], []
        for t in range(4):
            fresh = prop[o, 8 * t:8 * t + 8, :] * factor
            delta = fresh - prev[o, 8 * t:8 * t + 8, :]
            first = delta.astype(BF16).astype(F32)
            firsts.append(first)
            seconds.append(delta - first)
        for j in range(8):
            mask = highs[8 * o + j]
            for k, terms in enumerate((firsts, seconds)):
                block = jnp.concatenate([mask * term[j:j + 1, :] for term in terms], axis=0)
                amat[32 * k:32 * k + 32, 1024 * o + 128 * j:1024 * o + 128 * (j + 1)] = block.astype(BF16)
        if o % 4 == 3:
            span = slice(1024 * (o - 3), 1024 * (o + 1))
            part = jnp.dot(amat[:, span], lows[span, :], preferred_element_type=F32)
            acc = part if acc is None else acc + part

    cpart[...] = acc[32:64] + acc[0:32]
    remote(cpart, csib, 4, sibling)
    drain(cland.at[pl.ds(0, n_var - 1), own_rows, :], recv_sems.at[5])
    remote(cland.at[:, own_rows, :], cland.at[:, own_rows, :], 8, sibling)

    drain(cpart, recv_sems.at[4])
    coef[...] = cpart[...] + csib[...]
    wide = jnp.concatenate([coef[pl.ds(h, 4, stride=8), :] for h in range(8)], axis=1)
    coef_out[...] = wide
    offset = jnp.sum(wide * mean[...], axis=1, keepdims=True)
    pieces = jnp.concatenate(split3(wide), axis=0).astype(BF16)
    fitted = lax.dot_general(pieces, gb[...], (((1,), (1,)), ((), ())), preferred_element_type=F32)
    fitted = fitted[8:12] + fitted[4:8] + fitted[0:4] - offset
    lanes = people_dev // 128
    for k in range(lanes):
        pbuf[4 * k:4 * k + 4, :] = fitted[:, 128 * k:128 * (k + 1)]
    pland[v] = pbuf[...]
    for device in var_peers:
        remote(pland.at[v], pland.at[v], 6, device)

    @pl.when(jnp.logical_not(active))
    def _():
        drain(own, recv_sems.at[7])

    drain(cland.at[:, other_rows, :], recv_sems.at[8])
    own_table = jnp.broadcast_to(own[...], (8, 128))

    def renew(pair, carry):
        for k in range(2):
            slab = 2 * pair + k
            base = pl.multiple_of(slab * LIST_ROWS, 8)
            sources = snd[pl.ds(base + 32, 8), :].astype(jnp.int32)
            slots = snd[pl.ds(base + 40, 8), :].astype(jnp.int32)
            live = slots >= 0
            group = jnp.where(live, lax.shift_right_arithmetic(slots, 7), 0)
            factor = jnp.where(live, jnp.take_along_axis(own_table, group, axis=1), 0.0)
            high = lax.shift_right_arithmetic(sources, 7)
            low = lax.bitwise_and(sources, 127)
            for t in range(4):
                picked = jnp.zeros((8, 128), F32)
                for h in range(8):
                    row = jnp.broadcast_to(cland[slab, 8 * t + h:8 * t + h + 1, :], (8, 128))
                    picked = jnp.where(high == h, jnp.take_along_axis(row, low, axis=1), picked)
                old = snd[pl.ds(base + 8 * t, 8), :]
                fresh = (jnp.where(live, old, 0.0) + STEP * jnp.where(live, picked, 0.0)) * factor
                lat_out[t, pl.ds(pl.multiple_of(8 * slab, 8), 8), :] = fresh
        return carry

    lax.fori_loop(0, n_var // 2, renew, 0)

    drain(pland.at[pl.ds(0, n_var - 1)], recv_sems.at[6])
    predicted = pland[0]
    for k in range(1, n_var):
        predicted = predicted + pland[k]
    for k in range(lanes):
        res_out[:, 128 * k:128 * (k + 1)] = residual[:, 128 * k:128 * (k + 1)] - predicted[4 * k:4 * k + 4, :] * inverse_root

    drain(halves, send_sems.at[0])
    drain(win.at[pl.ds(0, 4 * reach - 1)], send_sems.at[1])
    drain(gland.at[pl.ds(0, n_var - 1)], send_sems.at[3])
    drain(cpart, send_sems.at[4])
    drain(cland.at[pl.ds(0, n_var - 1), own_rows, :], send_sems.at[5])
    drain(cland.at[:, own_rows, :], send_sems.at[8])
    drain(pland.at[pl.ds(0, n_var - 1)], send_sems.at[6])

    @pl.when(active)
    def _():
        drain(snd.at[pl.ds(0, LIST_ROWS * (n_var - 1)), :], send_sems.at[2])
        drain(own, send_sems.at[7])


def hand_out(lat, coef, res, lat_out, coef_out, res_out, sems):
    copies = [pltpu.make_async_copy(src, dst, sems.at[k])
              for k, (src, dst) in enumerate(((lat, lat_out), (coef, coef_out), (res, res_out)))]
    for copy in copies:
        copy.start()
    for copy in copies:
        copy.wait()


def per_device(n_people, n_var, genotype, dosage_mean, residual, latent_old, group_weight, copy_source, copy_slot):
    people_dev, var_dev = genotype.shape
    traits = residual.shape[0]
    inverse_root = 1.0 / math.sqrt(people_dev * n_people)
    half = n_var // 2
    n_z = n_people // 2
    list_rows = n_var * var_dev // 128
    vmem = pl.BlockSpec(memory_space=pltpu.VMEM)
    hbm = pl.BlockSpec(memory_space=pltpu.HBM)
    shapes = ((traits, list_rows, 128), (traits, var_dev), (traits, people_dev))
    held = pl.pallas_call(
        functools.partial(kernel, n_people, n_var, inverse_root),
        out_shape=tuple(pltpu.VMEM(shape, F32) for shape in shapes),
        in_specs=[hbm] * 7,
        out_specs=(vmem,) * 3,
        scratch_shapes=[
            pltpu.VMEM((people_dev, var_dev), jnp.int32),
            pltpu.VMEM((people_dev, var_dev), BF16),
            pltpu.VMEM((1, var_dev), F32),
            pltpu.VMEM((traits, people_dev), F32),
            pltpu.VMEM((traits, list_rows, 128), F32),
            pltpu.VMEM((1, 128), F32),
            pltpu.VMEM((n_var, 1024), jnp.int32),
            pltpu.VMEM((n_var, 1024), jnp.int32),
            pltpu.VMEM((n_var * LIST_ROWS, 128), F32),
            pltpu.VMEM((half, LIST_ROWS, 128), F32),
            pltpu.VMEM((32, 128), F32),
            pltpu.VMEM((n_z, 16, 128), F32),
            pltpu.VMEM((16, 128), F32),
            pltpu.VMEM((2, 32, 128), F32),
            pltpu.VMEM((32, 128), F32),
            pltpu.VMEM((32, 8, 128), F32),
            pltpu.VMEM((half * 128, 1024), BF16),
            pltpu.VMEM((half * 1024, 128), BF16),
            pltpu.VMEM((half * 8, 8, 128), F32),
            pltpu.VMEM((half, 32, 128), F32),
            pltpu.VMEM((half, 32, 128), F32),
            pltpu.VMEM((half * 8, 128), F32),
            pltpu.VMEM((n_var, half, 128), F32),
            pltpu.VMEM((half, 128), F32),
            pltpu.VMEM((64, half * 1024), BF16),
            pltpu.VMEM((n_var, 32, 128), F32),
            pltpu.VMEM((1, 128), F32),
            pltpu.VMEM((32, 128), F32),
            pltpu.VMEM((32, 128), F32),
            pltpu.VMEM((32, 128), F32),
            pltpu.VMEM((n_var, people_dev // 32, 128), F32),
            pltpu.VMEM((people_dev // 32, 128), F32),
            pltpu.SemaphoreType.DMA((10,)),
            pltpu.SemaphoreType.DMA((9,)),
            pltpu.SemaphoreType.DMA((9,)),
        ],
        compiler_params=pltpu.CompilerParams(collective_id=0, has_side_effects=True, vmem_limit_bytes=32 * 2**20),
    )(*(pltpu.with_memory_space_constraint(x, pltpu.HBM) for x in (
        genotype,
        dosage_mean.reshape(1, var_dev),
        residual,
        latent_old.reshape(traits, list_rows, 128),
        group_weight.reshape(1, 128),
        copy_source[0],
        copy_slot[0],
    )))
    lat, coef, res = pl.pallas_call(
        hand_out,
        out_shape=tuple(jax.ShapeDtypeStruct(shape, F32) for shape in shapes),
        in_specs=[vmem] * 3,
        out_specs=(hbm,) * 3,
        scratch_shapes=[pltpu.SemaphoreType.DMA((3,))],
    )(*(pltpu.with_memory_space_constraint(x, pltpu.VMEM) for x in held))
    return lat.reshape(latent_old.shape), coef, res


def solution(mesh):
    return jax.shard_map(
        functools.partial(per_device, mesh.shape["people"], mesh.shape["var"]),
        mesh=mesh,
        in_specs=(
            P("people", "var"),
            P("var"),
            P(None, "people"),
            P(None, "var", None),
            P("var"),
            P("var", None, None),
            P("var", None, None),
        ),
        out_specs=(P(None, "var", None), P(None, "var"), P(None, "people")),
        check_vma=False,
    )
```

```python
import functools
import math

import jax
import jax.numpy as jnp
from jax import lax
from jax.experimental import pallas as pl
from jax.experimental.pallas import tpu as pltpu
from jax.sharding import PartitionSpec as P

MESH = pl.DeviceIdType.MESH
F32 = jnp.float32
BF16 = jnp.bfloat16
STEP = 0.25
LIST_ROWS = 56


def split3(a):
    first = a.astype(BF16).astype(F32)
    rest = a - first
    second = rest.astype(BF16).astype(F32)
    return first, second, rest - second


def kernel(n_people, n_var, inverse_root,
           geno, mean_h, res_h, lat_h, weight_h, source_h, slot_h,
           lat_out, coef_out, res_out,
           gi, gb, mean, res, lat, weight, source, slot,
           snd, rcv, pc, spc, win, wsum, halves, corr, tables, member, lows,
           highs, prev, prop, squares, gland, thr, amat, cland, own,
           cpart, csib, coef, pland, pbuf,
           in_sems, send_sems, recv_sems):
    p, v = lax.axis_index("people"), lax.axis_index("var")
    n_z = n_people // 2
    core = lax.rem(p, 2)
    z = p // 2
    half = n_var // 2
    active = (v // half) == core
    sibling = {"people": p + 1 - 2 * core, "var": v}
    reach = n_z // 4

    def along(d, on):
        return {"people": 2 * lax.rem(z + d + n_z, n_z) + on, "var": v}

    near = sorted((d for d in range(-reach, reach + 1) if d != 0), key=lambda d: -abs(d))
    z_peers = [along(d, core) for d in near] + [along(d, 1 - core) for d in (reach, -reach)]
    side = math.isqrt(n_var)
    vy, vx = v // side, lax.rem(v, side)

    def in_plane(dy, dx):
        return {"people": p, "var": lax.rem(vy + dy, side) * side + lax.rem(vx + dx, side)}

    def hops(offset):
        return sum(min(d, side - d) for d in offset)

    offsets = [(dy, dx) for dy in range(side) for dx in range(side) if dy or dx]
    var_peers = [in_plane(dy, dx) for dy, dx in sorted(offsets, key=hops, reverse=True)]

    def local(src, dst, sem):
        copy = pltpu.make_async_copy(src, dst, sem)
        copy.start()
        return copy

    def remote(src, dst, k, device):
        copy = pltpu.make_async_remote_copy(src_ref=src, dst_ref=dst, send_sem=send_sems.at[k], recv_sem=recv_sems.at[k],
                                            device_id=device, device_id_type=MESH)
        copy.start()

    def drain(ref, sem):
        pltpu.make_async_copy(ref, ref, sem).wait()

    barrier = pltpu.get_barrier_semaphore()
    for device in z_peers + var_peers + [sibling]:
        pl.semaphore_signal(barrier, inc=1, device_id=device, device_id_type=MESH)

    people_dev = gi.shape[0]
    chunk = people_dev // 4
    small = [local(res_h, res, in_sems.at[4]), local(mean_h, mean, in_sems.at[5])]
    big = [local(geno.at[pl.ds(chunk * k, chunk), :], gi.at[pl.ds(chunk * k, chunk), :], in_sems.at[k]) for k in range(4)]
    lists = [local(lat_h, lat, in_sems.at[6]), local(weight_h, weight, in_sems.at[7]),
             local(source_h, source, in_sems.at[8]), local(slot_h, slot, in_sems.at[9])]

    for copy in small:
        copy.wait()
    residual = res[...]
    sums = jnp.sum(residual, axis=1, keepdims=True)
    parts = jnp.concatenate(split3(residual), axis=0).astype(BF16)
    total = None
    for k in range(4):
        big[k].wait()
        rows = pl.ds(chunk * k, chunk)
        block = gi[rows, :].astype(F32).astype(BF16)
        gb[rows, :] = block
        term = jnp.dot(parts[:, chunk * k:chunk * (k + 1)], block, preferred_element_type=F32)
        total = term if total is None else total + term
    products = total[8:12] + total[4:8] + total[0:4] - sums * mean[...]
    for h in range(8):
        pc[pl.ds(h, 4, stride=8), :] = products[:, 128 * h:128 * (h + 1)]

    for copy in lists:
        copy.wait()
    for i in range(n_var // 8):
        for j in range(8):
            block = pl.ds(8 * i * LIST_ROWS + 32 + j, 8, stride=LIST_ROWS)
            snd[block, :] = source[8 * i:8 * i + 8, 128 * j:128 * (j + 1)].astype(F32)
            block = pl.ds(8 * i * LIST_ROWS + 40 + j, 8, stride=LIST_ROWS)
            snd[block, :] = slot[8 * i:8 * i + 8, 128 * j:128 * (j + 1)].astype(F32)
    for s in range(n_var):
        for t in range(4):
            snd[LIST_ROWS * s + 8 * t:LIST_ROWS * s + 8 * t + 8, :] = lat[t, 8 * s:8 * s + 8, :]
        snd[LIST_ROWS * s + 48:LIST_ROWS * s + 56, :] = jnp.broadcast_to(weight[...], (8, 128))

    pl.semaphore_wait(barrier, len(z_peers) + len(var_peers) + 1)

    own_rows = pl.ds(pl.multiple_of(16 * core, 16), 16)
    other_rows = pl.ds(pl.multiple_of(16 - 16 * core, 16), 16)
    remote(pc.at[other_rows, :], spc, 9, sibling)
    def slab_rows(s):
        return pl.ds(pl.multiple_of(s * LIST_ROWS, 8), LIST_ROWS)

    mine = lax.rem(v, half)

    @pl.when(active)
    def _():
        for device in var_peers:
            remote(snd.at[slab_rows(device["var"]), :], rcv.at[mine], 2, device)
        rcv[mine] = snd[slab_rows(v), :]

    drain(spc, recv_sems.at[9])
    win[reach] = pc[own_rows, :] + spc[...]
    for d in near:
        if d < reach:
            remote(win.at[reach], win.at[reach + d], 1, along(-d, core))

    drain(win.at[pl.ds(0, 2 * reach - 1)], recv_sems.at[1])
    summed = win[0]
    for k in range(1, 2 * reach):
        summed = summed + win[k]
    wsum[...] = summed
    for k, d in enumerate((-reach, reach)):
        for on in (0, 1):
            remote(wsum, halves.at[k, own_rows, :], 0, along(d, on))

    @pl.when(active)
    def _():
        drain(rcv.at[pl.ds(0, half - 1)], recv_sems.at[2])

    @pl.when(jnp.logical_not(active))
    def _():
        drain(rcv, recv_sems.at[2])

    rows_iota = lax.broadcasted_iota(jnp.int32, (128, 128), 0)
    lanes_iota = lax.broadcasted_iota(jnp.int32, (128, 128), 1)
    hi_iota = lax.broadcasted_iota(jnp.int32, (8, 128), 0)

    def prepare(o, carry):
        sources = rcv[o, 32:40, :].astype(jnp.int32)
        slots = rcv[o, 40:48, :].astype(jnp.int32)
        live = slots >= 0
        group = jnp.where(live, lax.shift_right_arithmetic(slots, 7), -1)
        low = lax.bitwise_and(sources, 127)
        high = lax.shift_right_arithmetic(sources, 7)
        low_columns = low.T
        for j in range(8):
            rows = pl.ds(pl.multiple_of(128 * o, 128), 128)
            member[rows, 128 * j:128 * (j + 1)] = jnp.where(rows_iota == group[j:j + 1, :], 1.0, 0.0).astype(BF16)
            rows = pl.ds(pl.multiple_of(1024 * o + 128 * j, 128), 128)
            lows[rows, :] = jnp.where(lanes_iota == low_columns[:, j:j + 1], 1.0, 0.0).astype(BF16)
            highs[8 * o + j] = jnp.where(hi_iota == high[j:j + 1, :], 1.0, 0.0)
        for t in range(4):
            prev[o, 8 * t:8 * t + 8, :] = jnp.where(live, rcv[o, 8 * t:8 * t + 8, :], 0.0)
        thr[pl.ds(o, 1), :] = STEP * rcv[o, 48:49, :]
        return carry

    lax.fori_loop(0, half, prepare, 0)

    drain(halves, recv_sems.at[0])
    corr[...] = (halves[0] + halves[1]) * inverse_root
    for t in range(4):
        for h in range(8):
            tables[8 * t + h] = jnp.broadcast_to(corr[8 * t + h:8 * t + h + 1, :], (8, 128))

    for o in range(half):
        sources = rcv[o, 32:40, :].astype(jnp.int32)
        live = rcv[o, 40:48, :] >= 0.0
        high = lax.shift_right_arithmetic(sources, 7)
        low = lax.bitwise_and(sources, 127)
        total = jnp.zeros((8, 128), F32)
        for t in range(4):
            picked = jnp.zeros((8, 128), F32)
            for h in range(8):
                picked = jnp.where(high == h, jnp.take_along_axis(tables[8 * t + h], low, axis=1), picked)
            value = prev[o, 8 * t:8 * t + 8, :] + STEP * jnp.where(live, picked, 0.0)
            prop[o, 8 * t:8 * t + 8, :] = value
            total = total + value * value
        squares[8 * o:8 * o + 8, :] = total
    by_owner = jnp.concatenate([squares[pl.ds(j, half, stride=8), :] for j in range(8)], axis=1)
    stacked = jnp.concatenate(split3(by_owner), axis=0).astype(BF16)
    owner_iota = lax.broadcasted_iota(jnp.int32, (half, 128), 0)
    wide = lax.dot_general(stacked, member[...], (((1,), (1,)), ((), ())), preferred_element_type=F32)
    wide = wide[2 * half:3 * half] + wide[half:2 * half] + wide[0:half]
    partial = wide[:, 0:128]
    for o in range(1, half):
        partial = jnp.where(owner_iota == o, wide[:, 128 * o:128 * (o + 1)], partial)
    gland[v] = partial
    for device in var_peers:
        remote(gland.at[v], gland.at[v], 3, device)

    cland[v, own_rows, :] = corr[own_rows, :]
    for device in var_peers:
        remote(cland.at[v, own_rows, :], cland.at[v, own_rows, :], 5, device)
    drain(gland.at[pl.ds(0, n_var - 1)], recv_sems.at[3])
    norm = gland[0]
    for k in range(1, n_var):
        norm = norm + gland[k]
    norm = jnp.sqrt(norm)
    threshold = thr[...]
    shrink = jnp.maximum(norm - threshold, 0.0) / jnp.maximum(norm, threshold)
    squares[0:half, :] = shrink

    @pl.when(active)
    def _():
        own[...] = squares[pl.ds(mine, 1), :]
        remote(own, own, 7, sibling)

    acc = None
    for o in range(half):
        slots = rcv[o, 40:48, :].astype(jnp.int32)
        live = slots >= 0
        group = jnp.where(live, lax.shift_right_arithmetic(slots, 7), 0)
        table = jnp.broadcast_to(squares[o:o + 1, :], (8, 128))
        factor = jnp.where(live, jnp.take_along_axis(table, group, axis=1), 0.0)
        firsts, seconds = [], []
        for t in range(4):
            fresh = prop[o, 8 * t:8 * t + 8, :] * factor
            delta = fresh - prev[o, 8 * t:8 * t + 8, :]
            first = delta.astype(BF16).astype(F32)
            firsts.append(first)
            seconds.append(delta - first)
        for j in range(8):
            mask = highs[8 * o + j]
            for k, terms in enumerate((firsts, seconds)):
                block = jnp.concatenate([mask * term[j:j + 1, :] for term in terms], axis=0)
                amat[32 * k:32 * k + 32, 1024 * o + 128 * j:1024 * o + 128 * (j + 1)] = block.astype(BF16)
        if o % 4 == 3:
            span = slice(1024 * (o - 3), 1024 * (o + 1))
            part = jnp.dot(amat[:, span], lows[span, :], preferred_element_type=F32)
            acc = part if acc is None else acc + part

    cpart[...] = acc[32:64] + acc[0:32]
    remote(cpart, csib, 4, sibling)
    drain(cland.at[pl.ds(0, n_var - 1), own_rows, :], recv_sems.at[5])
    remote(cland.at[:, own_rows, :], cland.at[:, own_rows, :], 8, sibling)

    drain(cpart, recv_sems.at[4])
    coef[...] = cpart[...] + csib[...]
    wide = jnp.concatenate([coef[pl.ds(h, 4, stride=8), :] for h in range(8)], axis=1)
    coef_out[...] = wide
    offset = jnp.sum(wide * mean[...], axis=1, keepdims=True)
    pieces = jnp.concatenate(split3(wide), axis=0).astype(BF16)
    fitted = lax.dot_general(pieces, gb[...], (((1,), (1,)), ((), ())), preferred_element_type=F32)
    fitted = fitted[8:12] + fitted[4:8] + fitted[0:4] - offset
    lanes = people_dev // 128
    for k in range(lanes):
        pbuf[4 * k:4 * k + 4, :] = fitted[:, 128 * k:128 * (k + 1)]
    pland[v] = pbuf[...]
    for device in var_peers:
        remote(pland.at[v], pland.at[v], 6, device)

    @pl.when(jnp.logical_not(active))
    def _():
        drain(own, recv_sems.at[7])

    drain(cland.at[:, other_rows, :], recv_sems.at[8])
    own_table = jnp.broadcast_to(own[...], (8, 128))

    def renew(pair, carry):
        for k in range(2):
            slab = 2 * pair + k
            base = pl.multiple_of(slab * LIST_ROWS, 8)
            sources = snd[pl.ds(base + 32, 8), :].astype(jnp.int32)
            slots = snd[pl.ds(base + 40, 8), :].astype(jnp.int32)
            live = slots >= 0
            group = jnp.where(live, lax.shift_right_arithmetic(slots, 7), 0)
            factor = jnp.where(live, jnp.take_along_axis(own_table, group, axis=1), 0.0)
            high = lax.shift_right_arithmetic(sources, 7)
            low = lax.bitwise_and(sources, 127)
            for t in range(4):
                picked = jnp.zeros((8, 128), F32)
                for h in range(8):
                    row = jnp.broadcast_to(cland[slab, 8 * t + h:8 * t + h + 1, :], (8, 128))
                    picked = jnp.where(high == h, jnp.take_along_axis(row, low, axis=1), picked)
                old = snd[pl.ds(base + 8 * t, 8), :]
                fresh = (jnp.where(live, old, 0.0) + STEP * jnp.where(live, picked, 0.0)) * factor
                lat_out[t, pl.ds(pl.multiple_of(8 * slab, 8), 8), :] = fresh
        return carry

    lax.fori_loop(0, n_var // 2, renew, 0)

    drain(pland.at[pl.ds(0, n_var - 1)], recv_sems.at[6])
    predicted = pland[0]
    for k in range(1, n_var):
        predicted = predicted + pland[k]
    for k in range(lanes):
        res_out[:, 128 * k:128 * (k + 1)] = residual[:, 128 * k:128 * (k + 1)] - predicted[4 * k:4 * k + 4, :] * inverse_root

    drain(halves, send_sems.at[0])
    drain(spc, send_sems.at[9])
    drain(win.at[pl.ds(0, 2 * reach - 1)], send_sems.at[1])
    drain(gland.at[pl.ds(0, n_var - 1)], send_sems.at[3])
    drain(cpart, send_sems.at[4])
    drain(cland.at[pl.ds(0, n_var - 1), own_rows, :], send_sems.at[5])
    drain(cland.at[:, own_rows, :], send_sems.at[8])
    drain(pland.at[pl.ds(0, n_var - 1)], send_sems.at[6])

    @pl.when(active)
    def _():
        drain(snd.at[pl.ds(0, LIST_ROWS * (n_var - 1)), :], send_sems.at[2])
        drain(own, send_sems.at[7])


def hand_out(lat, coef, res, lat_out, coef_out, res_out, sems):
    copies = [pltpu.make_async_copy(src, dst, sems.at[k])
              for k, (src, dst) in enumerate(((lat, lat_out), (coef, coef_out), (res, res_out)))]
    for copy in copies:
        copy.start()
    for copy in copies:
        copy.wait()


def per_device(n_people, n_var, genotype, dosage_mean, residual, latent_old, group_weight, copy_source, copy_slot):
    people_dev, var_dev = genotype.shape
    traits = residual.shape[0]
    inverse_root = 1.0 / math.sqrt(people_dev * n_people)
    half = n_var // 2
    n_z = n_people // 2
    list_rows = n_var * var_dev // 128
    vmem = pl.BlockSpec(memory_space=pltpu.VMEM)
    hbm = pl.BlockSpec(memory_space=pltpu.HBM)
    shapes = ((traits, list_rows, 128), (traits, var_dev), (traits, people_dev))
    held = pl.pallas_call(
        functools.partial(kernel, n_people, n_var, inverse_root),
        out_shape=tuple(pltpu.VMEM(shape, F32) for shape in shapes),
        in_specs=[hbm] * 7,
        out_specs=(vmem,) * 3,
        scratch_shapes=[
            pltpu.VMEM((people_dev, var_dev), jnp.int32),
            pltpu.VMEM((people_dev, var_dev), BF16),
            pltpu.VMEM((1, var_dev), F32),
            pltpu.VMEM((traits, people_dev), F32),
            pltpu.VMEM((traits, list_rows, 128), F32),
            pltpu.VMEM((1, 128), F32),
            pltpu.VMEM((n_var, 1024), jnp.int32),
            pltpu.VMEM((n_var, 1024), jnp.int32),
            pltpu.VMEM((n_var * LIST_ROWS, 128), F32),
            pltpu.VMEM((half, LIST_ROWS, 128), F32),
            pltpu.VMEM((32, 128), F32),
            pltpu.VMEM((16, 128), F32),
            pltpu.VMEM((n_z // 2, 16, 128), F32),
            pltpu.VMEM((16, 128), F32),
            pltpu.VMEM((2, 32, 128), F32),
            pltpu.VMEM((32, 128), F32),
            pltpu.VMEM((32, 8, 128), F32),
            pltpu.VMEM((half * 128, 1024), BF16),
            pltpu.VMEM((half * 1024, 128), BF16),
            pltpu.VMEM((half * 8, 8, 128), F32),
            pltpu.VMEM((half, 32, 128), F32),
            pltpu.VMEM((half, 32, 128), F32),
            pltpu.VMEM((half * 8, 128), F32),
            pltpu.VMEM((n_var, half, 128), F32),
            pltpu.VMEM((half, 128), F32),
            pltpu.VMEM((64, half * 1024), BF16),
            pltpu.VMEM((n_var, 32, 128), F32),
            pltpu.VMEM((1, 128), F32),
            pltpu.VMEM((32, 128), F32),
            pltpu.VMEM((32, 128), F32),
            pltpu.VMEM((32, 128), F32),
            pltpu.VMEM((n_var, people_dev // 32, 128), F32),
            pltpu.VMEM((people_dev // 32, 128), F32),
            pltpu.SemaphoreType.DMA((10,)),
            pltpu.SemaphoreType.DMA((10,)),
            pltpu.SemaphoreType.DMA((10,)),
        ],
        compiler_params=pltpu.CompilerParams(collective_id=0, has_side_effects=True, vmem_limit_bytes=32 * 2**20),
    )(*(pltpu.with_memory_space_constraint(x, pltpu.HBM) for x in (
        genotype,
        dosage_mean.reshape(1, var_dev),
        residual,
        latent_old.reshape(traits, list_rows, 128),
        group_weight.reshape(1, 128),
        copy_source[0],
        copy_slot[0],
    )))
    lat, coef, res = pl.pallas_call(
        hand_out,
        out_shape=tuple(jax.ShapeDtypeStruct(shape, F32) for shape in shapes),
        in_specs=[vmem] * 3,
        out_specs=(hbm,) * 3,
        scratch_shapes=[pltpu.SemaphoreType.DMA((3,))],
    )(*(pltpu.with_memory_space_constraint(x, pltpu.VMEM) for x in held))
    return lat.reshape(latent_old.shape), coef, res


def solution(mesh):
    return jax.shard_map(
        functools.partial(per_device, mesh.shape["people"], mesh.shape["var"]),
        mesh=mesh,
        in_specs=(
            P("people", "var"),
            P("var"),
            P(None, "people"),
            P(None, "var", None),
            P("var"),
            P("var", None, None),
            P("var", None, None),
        ),
        out_specs=(P(None, "var", None), P(None, "var"), P(None, "people")),
        check_vma=False,
    )
```

```python
import functools
import math

import jax
import jax.numpy as jnp
from jax import lax
from jax.experimental import pallas as pl
from jax.experimental.pallas import tpu as pltpu
from jax.sharding import PartitionSpec as P

MESH = pl.DeviceIdType.MESH
F32 = jnp.float32
BF16 = jnp.bfloat16
STEP = 0.25
LIST_ROWS = 56


def split3(a):
    first = a.astype(BF16).astype(F32)
    rest = a - first
    second = rest.astype(BF16).astype(F32)
    return first, second, rest - second


def kernel(n_people, n_var, inverse_root,
           geno, mean_h, res_h, lat_h, weight_h, source_h, slot_h,
           lat_out, coef_out, res_out,
           gi, gb, mean, res, lat, weight, source, slot,
           snd, rcv, pc, spc, win, wsum, halves, corr, tables, member, lows,
           highs, prev, prop, squares, gland, thr, amat, cland, own,
           cpart, csib, coef, pland, pbuf,
           in_sems, send_sems, recv_sems):
    p, v = lax.axis_index("people"), lax.axis_index("var")
    n_z = n_people // 2
    core = lax.rem(p, 2)
    z = p // 2
    half = n_var // 2
    active = (v // half) == core
    sibling = {"people": p + 1 - 2 * core, "var": v}
    reach = n_z // 4

    def along(d, on):
        return {"people": 2 * lax.rem(z + d + n_z, n_z) + on, "var": v}

    near = sorted((d for d in range(-reach, reach + 1) if d != 0), key=lambda d: -abs(d))
    z_peers = [along(d, core) for d in near] + [along(d, 1 - core) for d in (reach, -reach)]
    side = math.isqrt(n_var)
    vy, vx = v // side, lax.rem(v, side)

    def in_plane(dy, dx):
        return {"people": p, "var": lax.rem(vy + dy, side) * side + lax.rem(vx + dx, side)}

    def hops(offset):
        return sum(min(d, side - d) for d in offset)

    offsets = [(dy, dx) for dy in range(side) for dx in range(side) if dy or dx]
    var_peers = [in_plane(dy, dx) for dy, dx in sorted(offsets, key=hops, reverse=True)]

    def local(src, dst, sem):
        copy = pltpu.make_async_copy(src, dst, sem)
        copy.start()
        return copy

    def remote(src, dst, k, device):
        copy = pltpu.make_async_remote_copy(src_ref=src, dst_ref=dst, send_sem=send_sems.at[k], recv_sem=recv_sems.at[k],
                                            device_id=device, device_id_type=MESH)
        copy.start()

    def drain(ref, sem):
        pltpu.make_async_copy(ref, ref, sem).wait()

    barrier = pltpu.get_barrier_semaphore()
    for device in z_peers + var_peers + [sibling]:
        pl.semaphore_signal(barrier, inc=1, device_id=device, device_id_type=MESH)

    people_dev = gi.shape[0]
    chunk = people_dev // 4
    small = [local(res_h, res, in_sems.at[4]), local(mean_h, mean, in_sems.at[5])]
    big = [local(geno.at[pl.ds(chunk * k, chunk), :], gi.at[pl.ds(chunk * k, chunk), :], in_sems.at[k]) for k in range(4)]
    lists = [local(lat_h, lat, in_sems.at[6]), local(weight_h, weight, in_sems.at[7]),
             local(source_h, source, in_sems.at[8]), local(slot_h, slot, in_sems.at[9])]

    for copy in small:
        copy.wait()
    residual = res[...]
    sums = jnp.sum(residual, axis=1, keepdims=True)
    parts = jnp.concatenate(split3(residual), axis=0).astype(BF16)
    total = None
    for k in range(4):
        big[k].wait()
        rows = pl.ds(chunk * k, chunk)
        block = gi[rows, :].astype(F32).astype(BF16)
        gb[rows, :] = block
        term = jnp.dot(parts[:, chunk * k:chunk * (k + 1)], block, preferred_element_type=F32)
        total = term if total is None else total + term
    products = total[8:12] + total[4:8] + total[0:4] - sums * mean[...]
    for h in range(8):
        pc[pl.ds(h, 4, stride=8), :] = products[:, 128 * h:128 * (h + 1)]

    for copy in lists:
        copy.wait()
    for i in range(n_var // 8):
        for j in range(8):
            block = pl.ds(8 * i * LIST_ROWS + 32 + j, 8, stride=LIST_ROWS)
            snd[block, :] = source[8 * i:8 * i + 8, 128 * j:128 * (j + 1)].astype(F32)
            block = pl.ds(8 * i * LIST_ROWS + 40 + j, 8, stride=LIST_ROWS)
            snd[block, :] = slot[8 * i:8 * i + 8, 128 * j:128 * (j + 1)].astype(F32)
    for s in range(n_var):
        for t in range(4):
            snd[LIST_ROWS * s + 8 * t:LIST_ROWS * s + 8 * t + 8, :] = lat[t, 8 * s:8 * s + 8, :]
        snd[LIST_ROWS * s + 48:LIST_ROWS * s + 56, :] = jnp.broadcast_to(weight[...], (8, 128))

    pl.semaphore_wait(barrier, len(z_peers) + len(var_peers) + 1)

    own_rows = pl.ds(pl.multiple_of(16 * core, 16), 16)
    other_rows = pl.ds(pl.multiple_of(16 - 16 * core, 16), 16)
    remote(pc.at[other_rows, :], spc, 9, sibling)
    def slab_rows(s):
        return pl.ds(pl.multiple_of(s * LIST_ROWS, 8), LIST_ROWS)

    mine = lax.rem(v, half)

    @pl.when(active)
    def _():
        for device in var_peers:
            remote(snd.at[slab_rows(device["var"]), :], rcv.at[mine], 2, device)
        rcv[mine] = snd[slab_rows(v), :]

    drain(spc, recv_sems.at[9])
    win[reach] = pc[own_rows, :] + spc[...]
    for d in near:
        if d < reach:
            remote(win.at[reach], win.at[reach + d], 1, along(-d, core))

    drain(win.at[pl.ds(0, 2 * reach - 1)], recv_sems.at[1])
    summed = win[0]
    for k in range(1, 2 * reach):
        summed = summed + win[k]
    wsum[...] = summed
    for k, d in enumerate((-reach, reach)):
        for on in (0, 1):
            remote(wsum, halves.at[k, own_rows, :], 0, along(d, on))

    @pl.when(active)
    def _():
        drain(rcv.at[pl.ds(0, half - 1)], recv_sems.at[2])

    @pl.when(jnp.logical_not(active))
    def _():
        drain(rcv, recv_sems.at[2])

    rows_iota = lax.broadcasted_iota(jnp.int32, (128, 128), 0)
    lanes_iota = lax.broadcasted_iota(jnp.int32, (128, 128), 1)
    hi_iota = lax.broadcasted_iota(jnp.int32, (8, 128), 0)

    def prepare(o, carry):
        sources = rcv[o, 32:40, :].astype(jnp.int32)
        slots = rcv[o, 40:48, :].astype(jnp.int32)
        live = slots >= 0
        group = jnp.where(live, lax.shift_right_arithmetic(slots, 7), -1)
        low = lax.bitwise_and(sources, 127)
        high = lax.shift_right_arithmetic(sources, 7)
        low_columns = low.T
        for j in range(8):
            rows = pl.ds(pl.multiple_of(128 * o, 128), 128)
            member[rows, 128 * j:128 * (j + 1)] = jnp.where(rows_iota == group[j:j + 1, :], 1.0, 0.0).astype(BF16)
            rows = pl.ds(pl.multiple_of(1024 * o + 128 * j, 128), 128)
            lows[rows, :] = jnp.where(lanes_iota == low_columns[:, j:j + 1], 1.0, 0.0).astype(BF16)
            highs[8 * o + j] = jnp.where(hi_iota == high[j:j + 1, :], 1.0, 0.0)
        for t in range(4):
            prev[o, 8 * t:8 * t + 8, :] = jnp.where(live, rcv[o, 8 * t:8 * t + 8, :], 0.0)
        thr[pl.ds(o, 1), :] = STEP * rcv[o, 48:49, :]
        return carry

    lax.fori_loop(0, half, prepare, 0)

    drain(halves, recv_sems.at[0])
    corr[...] = (halves[0] + halves[1]) * inverse_root
    cland[v, own_rows, :] = corr[own_rows, :]
    for device in var_peers:
        remote(cland.at[v, own_rows, :], cland.at[v, own_rows, :], 5, device)
    for t in range(4):
        for h in range(8):
            tables[8 * t + h] = jnp.broadcast_to(corr[8 * t + h:8 * t + h + 1, :], (8, 128))

    for o in range(half):
        sources = rcv[o, 32:40, :].astype(jnp.int32)
        live = rcv[o, 40:48, :] >= 0.0
        high = lax.shift_right_arithmetic(sources, 7)
        low = lax.bitwise_and(sources, 127)
        total = jnp.zeros((8, 128), F32)
        for t in range(4):
            picked = jnp.zeros((8, 128), F32)
            for h in range(8):
                picked = jnp.where(high == h, jnp.take_along_axis(tables[8 * t + h], low, axis=1), picked)
            value = prev[o, 8 * t:8 * t + 8, :] + STEP * jnp.where(live, picked, 0.0)
            prop[o, 8 * t:8 * t + 8, :] = value
            total = total + value * value
        squares[8 * o:8 * o + 8, :] = total
    by_owner = jnp.concatenate([squares[pl.ds(j, half, stride=8), :] for j in range(8)], axis=1)
    stacked = jnp.concatenate(split3(by_owner), axis=0).astype(BF16)
    owner_iota = lax.broadcasted_iota(jnp.int32, (half, 128), 0)
    wide = lax.dot_general(stacked, member[...], (((1,), (1,)), ((), ())), preferred_element_type=F32)
    wide = wide[2 * half:3 * half] + wide[half:2 * half] + wide[0:half]
    partial = wide[:, 0:128]
    for o in range(1, half):
        partial = jnp.where(owner_iota == o, wide[:, 128 * o:128 * (o + 1)], partial)
    gland[v] = partial
    for device in var_peers:
        remote(gland.at[v], gland.at[v], 3, device)
    drain(gland.at[pl.ds(0, n_var - 1)], recv_sems.at[3])
    norm = gland[0]
    for k in range(1, n_var):
        norm = norm + gland[k]
    norm = jnp.sqrt(norm)
    threshold = thr[...]
    shrink = jnp.maximum(norm - threshold, 0.0) / jnp.maximum(norm, threshold)
    squares[0:half, :] = shrink

    @pl.when(active)
    def _():
        own[...] = squares[pl.ds(mine, 1), :]
        remote(own, own, 7, sibling)

    acc = None
    for o in range(half):
        slots = rcv[o, 40:48, :].astype(jnp.int32)
        live = slots >= 0
        group = jnp.where(live, lax.shift_right_arithmetic(slots, 7), 0)
        table = jnp.broadcast_to(squares[o:o + 1, :], (8, 128))
        factor = jnp.where(live, jnp.take_along_axis(table, group, axis=1), 0.0)
        firsts, seconds = [], []
        for t in range(4):
            fresh = prop[o, 8 * t:8 * t + 8, :] * factor
            delta = fresh - prev[o, 8 * t:8 * t + 8, :]
            first = delta.astype(BF16).astype(F32)
            firsts.append(first)
            seconds.append(delta - first)
        for j in range(8):
            mask = highs[8 * o + j]
            for k, terms in enumerate((firsts, seconds)):
                block = jnp.concatenate([mask * term[j:j + 1, :] for term in terms], axis=0)
                amat[32 * k:32 * k + 32, 1024 * o + 128 * j:1024 * o + 128 * (j + 1)] = block.astype(BF16)
        if o % 4 == 3:
            span = slice(1024 * (o - 3), 1024 * (o + 1))
            part = jnp.dot(amat[:, span], lows[span, :], preferred_element_type=F32)
            acc = part if acc is None else acc + part

    cpart[...] = acc[32:64] + acc[0:32]
    remote(cpart, csib, 4, sibling)
    drain(cland.at[pl.ds(0, n_var - 1), own_rows, :], recv_sems.at[5])
    remote(cland.at[:, own_rows, :], cland.at[:, own_rows, :], 8, sibling)

    drain(cpart, recv_sems.at[4])
    coef[...] = cpart[...] + csib[...]
    wide = jnp.concatenate([coef[pl.ds(h, 4, stride=8), :] for h in range(8)], axis=1)
    coef_out[...] = wide
    offset = jnp.sum(wide * mean[...], axis=1, keepdims=True)
    pieces = jnp.concatenate(split3(wide), axis=0).astype(BF16)
    fitted = lax.dot_general(pieces, gb[...], (((1,), (1,)), ((), ())), preferred_element_type=F32)
    fitted = fitted[8:12] + fitted[4:8] + fitted[0:4] - offset
    lanes = people_dev // 128
    for k in range(lanes):
        pbuf[4 * k:4 * k + 4, :] = fitted[:, 128 * k:128 * (k + 1)]
    pland[v] = pbuf[...]
    for device in var_peers:
        remote(pland.at[v], pland.at[v], 6, device)

    @pl.when(jnp.logical_not(active))
    def _():
        drain(own, recv_sems.at[7])

    drain(cland.at[:, other_rows, :], recv_sems.at[8])
    own_table = jnp.broadcast_to(own[...], (8, 128))

    def renew(pair, carry):
        for k in range(2):
            slab = 2 * pair + k
            base = pl.multiple_of(slab * LIST_ROWS, 8)
            sources = snd[pl.ds(base + 32, 8), :].astype(jnp.int32)
            slots = snd[pl.ds(base + 40, 8), :].astype(jnp.int32)
            live = slots >= 0
            group = jnp.where(live, lax.shift_right_arithmetic(slots, 7), 0)
            factor = jnp.where(live, jnp.take_along_axis(own_table, group, axis=1), 0.0)
            high = lax.shift_right_arithmetic(sources, 7)
            low = lax.bitwise_and(sources, 127)
            for t in range(4):
                picked = jnp.zeros((8, 128), F32)
                for h in range(8):
                    row = jnp.broadcast_to(cland[slab, 8 * t + h:8 * t + h + 1, :], (8, 128))
                    picked = jnp.where(high == h, jnp.take_along_axis(row, low, axis=1), picked)
                old = snd[pl.ds(base + 8 * t, 8), :]
                fresh = (jnp.where(live, old, 0.0) + STEP * jnp.where(live, picked, 0.0)) * factor
                lat_out[t, pl.ds(pl.multiple_of(8 * slab, 8), 8), :] = fresh
        return carry

    lax.fori_loop(0, n_var // 2, renew, 0)

    drain(pland.at[pl.ds(0, n_var - 1)], recv_sems.at[6])
    predicted = pland[0]
    for k in range(1, n_var):
        predicted = predicted + pland[k]
    for k in range(lanes):
        res_out[:, 128 * k:128 * (k + 1)] = residual[:, 128 * k:128 * (k + 1)] - predicted[4 * k:4 * k + 4, :] * inverse_root

    drain(halves, send_sems.at[0])
    drain(spc, send_sems.at[9])
    drain(win.at[pl.ds(0, 2 * reach - 1)], send_sems.at[1])
    drain(gland.at[pl.ds(0, n_var - 1)], send_sems.at[3])
    drain(cpart, send_sems.at[4])
    drain(cland.at[pl.ds(0, n_var - 1), own_rows, :], send_sems.at[5])
    drain(cland.at[:, own_rows, :], send_sems.at[8])
    drain(pland.at[pl.ds(0, n_var - 1)], send_sems.at[6])

    @pl.when(active)
    def _():
        drain(snd.at[pl.ds(0, LIST_ROWS * (n_var - 1)), :], send_sems.at[2])
        drain(own, send_sems.at[7])


def hand_out(lat, coef, res, lat_out, coef_out, res_out, sems):
    copies = [pltpu.make_async_copy(src, dst, sems.at[k])
              for k, (src, dst) in enumerate(((lat, lat_out), (coef, coef_out), (res, res_out)))]
    for copy in copies:
        copy.start()
    for copy in copies:
        copy.wait()


def per_device(n_people, n_var, genotype, dosage_mean, residual, latent_old, group_weight, copy_source, copy_slot):
    people_dev, var_dev = genotype.shape
    traits = residual.shape[0]
    inverse_root = 1.0 / math.sqrt(people_dev * n_people)
    half = n_var // 2
    n_z = n_people // 2
    list_rows = n_var * var_dev // 128
    vmem = pl.BlockSpec(memory_space=pltpu.VMEM)
    hbm = pl.BlockSpec(memory_space=pltpu.HBM)
    shapes = ((traits, list_rows, 128), (traits, var_dev), (traits, people_dev))
    held = pl.pallas_call(
        functools.partial(kernel, n_people, n_var, inverse_root),
        out_shape=tuple(pltpu.VMEM(shape, F32) for shape in shapes),
        in_specs=[hbm] * 7,
        out_specs=(vmem,) * 3,
        scratch_shapes=[
            pltpu.VMEM((people_dev, var_dev), jnp.int32),
            pltpu.VMEM((people_dev, var_dev), BF16),
            pltpu.VMEM((1, var_dev), F32),
            pltpu.VMEM((traits, people_dev), F32),
            pltpu.VMEM((traits, list_rows, 128), F32),
            pltpu.VMEM((1, 128), F32),
            pltpu.VMEM((n_var, 1024), jnp.int32),
            pltpu.VMEM((n_var, 1024), jnp.int32),
            pltpu.VMEM((n_var * LIST_ROWS, 128), F32),
            pltpu.VMEM((half, LIST_ROWS, 128), F32),
            pltpu.VMEM((32, 128), F32),
            pltpu.VMEM((16, 128), F32),
            pltpu.VMEM((n_z // 2, 16, 128), F32),
            pltpu.VMEM((16, 128), F32),
            pltpu.VMEM((2, 32, 128), F32),
            pltpu.VMEM((32, 128), F32),
            pltpu.VMEM((32, 8, 128), F32),
            pltpu.VMEM((half * 128, 1024), BF16),
            pltpu.VMEM((half * 1024, 128), BF16),
            pltpu.VMEM((half * 8, 8, 128), F32),
            pltpu.VMEM((half, 32, 128), F32),
            pltpu.VMEM((half, 32, 128), F32),
            pltpu.VMEM((half * 8, 128), F32),
            pltpu.VMEM((n_var, half, 128), F32),
            pltpu.VMEM((half, 128), F32),
            pltpu.VMEM((64, half * 1024), BF16),
            pltpu.VMEM((n_var, 32, 128), F32),
            pltpu.VMEM((1, 128), F32),
            pltpu.VMEM((32, 128), F32),
            pltpu.VMEM((32, 128), F32),
            pltpu.VMEM((32, 128), F32),
            pltpu.VMEM((n_var, people_dev // 32, 128), F32),
            pltpu.VMEM((people_dev // 32, 128), F32),
            pltpu.SemaphoreType.DMA((10,)),
            pltpu.SemaphoreType.DMA((10,)),
            pltpu.SemaphoreType.DMA((10,)),
        ],
        compiler_params=pltpu.CompilerParams(collective_id=0, has_side_effects=True, vmem_limit_bytes=32 * 2**20),
    )(*(pltpu.with_memory_space_constraint(x, pltpu.HBM) for x in (
        genotype,
        dosage_mean.reshape(1, var_dev),
        residual,
        latent_old.reshape(traits, list_rows, 128),
        group_weight.reshape(1, 128),
        copy_source[0],
        copy_slot[0],
    )))
    lat, coef, res = pl.pallas_call(
        hand_out,
        out_shape=tuple(jax.ShapeDtypeStruct(shape, F32) for shape in shapes),
        in_specs=[vmem] * 3,
        out_specs=(hbm,) * 3,
        scratch_shapes=[pltpu.SemaphoreType.DMA((3,))],
    )(*(pltpu.with_memory_space_constraint(x, pltpu.VMEM) for x in held))
    return lat.reshape(latent_old.shape), coef, res


def solution(mesh):
    return jax.shard_map(
        functools.partial(per_device, mesh.shape["people"], mesh.shape["var"]),
        mesh=mesh,
        in_specs=(
            P("people", "var"),
            P("var"),
            P(None, "people"),
            P(None, "var", None),
            P("var"),
            P("var", None, None),
            P("var", None, None),
        ),
        out_specs=(P(None, "var", None), P(None, "var"), P(None, "people")),
        check_vma=False,
    )
```

```python
import functools
import math

import jax
import jax.numpy as jnp
from jax import lax
from jax.experimental import pallas as pl
from jax.experimental.pallas import tpu as pltpu
from jax.sharding import PartitionSpec as P

MESH = pl.DeviceIdType.MESH
F32 = jnp.float32
BF16 = jnp.bfloat16
STEP = 0.25
LIST_ROWS = 56


def split3(a):
    first = a.astype(BF16).astype(F32)
    rest = a - first
    second = rest.astype(BF16).astype(F32)
    return first, second, rest - second


def kernel(n_people, n_var, inverse_root,
           geno, mean_h, res_h, lat_h, weight_h, source_h, slot_h,
           lat_out, coef_out, res_out,
           gi, gb, mean, res, lat, weight, source, slot,
           snd, rcv, pc, spc, win, wsum, halves, corr, tables, member, lows,
           highs, prev, prop, squares, gland, thr, amat, cland, own,
           cpart, csib, coef, pland, pbuf,
           in_sems, send_sems, recv_sems):
    p, v = lax.axis_index("people"), lax.axis_index("var")
    n_z = n_people // 2
    core = lax.rem(p, 2)
    z = p // 2
    half = n_var // 2
    active = (v // half) == core
    sibling = {"people": p + 1 - 2 * core, "var": v}
    reach = n_z // 4

    def along(d, on):
        return {"people": 2 * lax.rem(z + d + n_z, n_z) + on, "var": v}

    near = sorted((d for d in range(-reach, reach + 1) if d != 0), key=lambda d: -abs(d))
    z_peers = [along(d, core) for d in near] + [along(d, 1 - core) for d in (reach, -reach)]
    side = math.isqrt(n_var)
    vy, vx = v // side, lax.rem(v, side)

    def in_plane(dy, dx):
        return {"people": p, "var": lax.rem(vy + dy, side) * side + lax.rem(vx + dx, side)}

    def hops(offset):
        return sum(min(d, side - d) for d in offset)

    offsets = [(dy, dx) for dy in range(side) for dx in range(side) if dy or dx]
    var_peers = [in_plane(dy, dx) for dy, dx in sorted(offsets, key=hops, reverse=True)]

    def local(src, dst, sem):
        copy = pltpu.make_async_copy(src, dst, sem)
        copy.start()
        return copy

    def remote(src, dst, k, device):
        copy = pltpu.make_async_remote_copy(src_ref=src, dst_ref=dst, send_sem=send_sems.at[k], recv_sem=recv_sems.at[k],
                                            device_id=device, device_id_type=MESH)
        copy.start()

    def drain(ref, sem):
        pltpu.make_async_copy(ref, ref, sem).wait()

    barrier = pltpu.get_barrier_semaphore()
    for device in z_peers + var_peers + [sibling]:
        pl.semaphore_signal(barrier, inc=1, device_id=device, device_id_type=MESH)

    people_dev = gi.shape[0]
    chunk = people_dev // 4
    small = [local(res_h, res, in_sems.at[4]), local(mean_h, mean, in_sems.at[5])]
    big = [local(geno.at[pl.ds(chunk * k, chunk), :], gi.at[pl.ds(chunk * k, chunk), :], in_sems.at[k]) for k in range(4)]
    lists = [local(lat_h, lat, in_sems.at[6]), local(weight_h, weight, in_sems.at[7]),
             local(source_h, source, in_sems.at[8]), local(slot_h, slot, in_sems.at[9])]

    for copy in small:
        copy.wait()
    residual = res[...]
    sums = jnp.sum(residual, axis=1, keepdims=True)
    parts = jnp.concatenate(split3(residual), axis=0).astype(BF16)
    total = None
    for k in range(4):
        big[k].wait()
        rows = pl.ds(chunk * k, chunk)
        block = gi[rows, :].astype(F32).astype(BF16)
        gb[rows, :] = block
        term = jnp.dot(parts[:, chunk * k:chunk * (k + 1)], block, preferred_element_type=F32)
        total = term if total is None else total + term
    products = total[8:12] + total[4:8] + total[0:4] - sums * mean[...]
    for h in range(8):
        pc[pl.ds(h, 4, stride=8), :] = products[:, 128 * h:128 * (h + 1)]

    for copy in lists:
        copy.wait()
    for i in range(n_var // 8):
        for j in range(8):
            block = pl.ds(8 * i * LIST_ROWS + 32 + j, 8, stride=LIST_ROWS)
            snd[block, :] = source[8 * i:8 * i + 8, 128 * j:128 * (j + 1)].astype(F32)
            block = pl.ds(8 * i * LIST_ROWS + 40 + j, 8, stride=LIST_ROWS)
            snd[block, :] = slot[8 * i:8 * i + 8, 128 * j:128 * (j + 1)].astype(F32)
    for s in range(n_var):
        for t in range(4):
            snd[LIST_ROWS * s + 8 * t:LIST_ROWS * s + 8 * t + 8, :] = lat[t, 8 * s:8 * s + 8, :]
        snd[LIST_ROWS * s + 48:LIST_ROWS * s + 56, :] = jnp.broadcast_to(weight[...], (8, 128))

    pl.semaphore_wait(barrier, len(z_peers) + len(var_peers) + 1)

    own_rows = pl.ds(pl.multiple_of(16 * core, 16), 16)
    other_rows = pl.ds(pl.multiple_of(16 - 16 * core, 16), 16)
    remote(pc.at[other_rows, :], spc, 9, sibling)
    def slab_rows(s):
        return pl.ds(pl.multiple_of(s * LIST_ROWS, 8), LIST_ROWS)

    mine = lax.rem(v, half)

    @pl.when(active)
    def _():
        for device in var_peers:
            remote(snd.at[slab_rows(device["var"]), :], rcv.at[mine], 2, device)
        rcv[mine] = snd[slab_rows(v), :]

    drain(spc, recv_sems.at[9])
    win[reach] = pc[own_rows, :] + spc[...]
    for d in near:
        if d < reach:
            remote(win.at[reach], win.at[reach + d], 1, along(-d, core))

    drain(win.at[pl.ds(0, 2 * reach - 1)], recv_sems.at[1])
    summed = win[0]
    for k in range(1, 2 * reach):
        summed = summed + win[k]
    wsum[...] = summed
    for k, d in enumerate((-reach, reach)):
        for on in (0, 1):
            remote(wsum, halves.at[k, own_rows, :], 0, along(d, on))

    @pl.when(active)
    def _():
        drain(rcv.at[pl.ds(0, half - 1)], recv_sems.at[2])

    @pl.when(jnp.logical_not(active))
    def _():
        drain(rcv, recv_sems.at[2])

    rows_iota = lax.broadcasted_iota(jnp.int32, (128, 128), 0)
    lanes_iota = lax.broadcasted_iota(jnp.int32, (128, 128), 1)
    hi_iota = lax.broadcasted_iota(jnp.int32, (8, 128), 0)

    def prepare(o, carry):
        sources = rcv[o, 32:40, :].astype(jnp.int32)
        slots = rcv[o, 40:48, :].astype(jnp.int32)
        live = slots >= 0
        group = jnp.where(live, lax.shift_right_arithmetic(slots, 7), -1)
        low = lax.bitwise_and(sources, 127)
        high = lax.shift_right_arithmetic(sources, 7)
        low_columns = low.T
        for j in range(8):
            rows = pl.ds(pl.multiple_of(128 * o, 128), 128)
            member[rows, 128 * j:128 * (j + 1)] = jnp.where(rows_iota == group[j:j + 1, :], 1.0, 0.0).astype(BF16)
            rows = pl.ds(pl.multiple_of(1024 * o + 128 * j, 128), 128)
            lows[rows, :] = jnp.where(lanes_iota == low_columns[:, j:j + 1], 1.0, 0.0).astype(BF16)
            highs[8 * o + j] = jnp.where(hi_iota == high[j:j + 1, :], 1.0, 0.0)
        for t in range(4):
            prev[o, 8 * t:8 * t + 8, :] = jnp.where(live, rcv[o, 8 * t:8 * t + 8, :], 0.0)
        thr[pl.ds(o, 1), :] = STEP * rcv[o, 48:49, :]
        return carry

    lax.fori_loop(0, half, prepare, 0)

    drain(halves, recv_sems.at[0])
    corr[...] = (halves[0] + halves[1]) * inverse_root
    cland[v, own_rows, :] = corr[own_rows, :]
    for device in var_peers:
        remote(cland.at[v, own_rows, :], cland.at[v, own_rows, :], 5, device)
    for t in range(4):
        for h in range(8):
            tables[8 * t + h] = jnp.broadcast_to(corr[8 * t + h:8 * t + h + 1, :], (8, 128))

    owner_iota = lax.broadcasted_iota(jnp.int32, (4, 128), 0)
    for o in range(half):
        sources = rcv[o, 32:40, :].astype(jnp.int32)
        live = rcv[o, 40:48, :] >= 0.0
        high = lax.shift_right_arithmetic(sources, 7)
        low = lax.bitwise_and(sources, 127)
        total = jnp.zeros((8, 128), F32)
        for t in range(4):
            picked = jnp.zeros((8, 128), F32)
            for h in range(8):
                picked = jnp.where(high == h, jnp.take_along_axis(tables[8 * t + h], low, axis=1), picked)
            value = prev[o, 8 * t:8 * t + 8, :] + STEP * jnp.where(live, picked, 0.0)
            prop[o, 8 * t:8 * t + 8, :] = value
            total = total + value * value
        squares[8 * o:8 * o + 8, :] = total
        if o % 4 == 3:
            base = o - 3
            by_owner = jnp.concatenate([squares[pl.ds(8 * base + j, 4, stride=8), :] for j in range(8)], axis=1)
            stacked = jnp.concatenate(split3(by_owner), axis=0).astype(BF16)
            wide = lax.dot_general(stacked, member[128 * base:128 * (base + 4), :], (((1,), (1,)), ((), ())),
                                   preferred_element_type=F32)
            wide = wide[8:12] + wide[4:8] + wide[0:4]
            partial = wide[:, 0:128]
            for k in range(1, 4):
                partial = jnp.where(owner_iota == k, wide[:, 128 * k:128 * (k + 1)], partial)
            gland[v, base:base + 4, :] = partial
    for device in var_peers:
        remote(gland.at[v], gland.at[v], 3, device)
    drain(gland.at[pl.ds(0, n_var - 1)], recv_sems.at[3])
    norm = gland[0]
    for k in range(1, n_var):
        norm = norm + gland[k]
    norm = jnp.sqrt(norm)
    threshold = thr[...]
    shrink = jnp.maximum(norm - threshold, 0.0) / jnp.maximum(norm, threshold)
    squares[0:half, :] = shrink

    @pl.when(active)
    def _():
        own[...] = squares[pl.ds(mine, 1), :]
        remote(own, own, 7, sibling)

    acc = None
    for o in range(half):
        slots = rcv[o, 40:48, :].astype(jnp.int32)
        live = slots >= 0
        group = jnp.where(live, lax.shift_right_arithmetic(slots, 7), 0)
        table = jnp.broadcast_to(squares[o:o + 1, :], (8, 128))
        factor = jnp.where(live, jnp.take_along_axis(table, group, axis=1), 0.0)
        firsts, seconds = [], []
        for t in range(4):
            fresh = prop[o, 8 * t:8 * t + 8, :] * factor
            delta = fresh - prev[o, 8 * t:8 * t + 8, :]
            first = delta.astype(BF16).astype(F32)
            firsts.append(first)
            seconds.append(delta - first)
        for j in range(8):
            mask = highs[8 * o + j]
            for k, terms in enumerate((firsts, seconds)):
                block = jnp.concatenate([mask * term[j:j + 1, :] for term in terms], axis=0)
                amat[32 * k:32 * k + 32, 1024 * o + 128 * j:1024 * o + 128 * (j + 1)] = block.astype(BF16)
        if o % 4 == 3:
            span = slice(1024 * (o - 3), 1024 * (o + 1))
            part = jnp.dot(amat[:, span], lows[span, :], preferred_element_type=F32)
            acc = part if acc is None else acc + part

    cpart[...] = acc[32:64] + acc[0:32]
    remote(cpart, csib, 4, sibling)
    drain(cland.at[pl.ds(0, n_var - 1), own_rows, :], recv_sems.at[5])
    remote(cland.at[:, own_rows, :], cland.at[:, own_rows, :], 8, sibling)

    drain(cpart, recv_sems.at[4])
    coef[...] = cpart[...] + csib[...]
    wide = jnp.concatenate([coef[pl.ds(h, 4, stride=8), :] for h in range(8)], axis=1)
    coef_out[...] = wide
    offset = jnp.sum(wide * mean[...], axis=1, keepdims=True)
    pieces = jnp.concatenate(split3(wide), axis=0).astype(BF16)
    fitted = lax.dot_general(pieces, gb[...], (((1,), (1,)), ((), ())), preferred_element_type=F32)
    fitted = fitted[8:12] + fitted[4:8] + fitted[0:4] - offset
    lanes = people_dev // 128
    for k in range(lanes):
        pbuf[4 * k:4 * k + 4, :] = fitted[:, 128 * k:128 * (k + 1)]
    pland[v] = pbuf[...]
    for device in var_peers:
        remote(pland.at[v], pland.at[v], 6, device)

    @pl.when(jnp.logical_not(active))
    def _():
        drain(own, recv_sems.at[7])

    drain(cland.at[:, other_rows, :], recv_sems.at[8])
    own_table = jnp.broadcast_to(own[...], (8, 128))

    def renew(pair, carry):
        for k in range(2):
            slab = 2 * pair + k
            base = pl.multiple_of(slab * LIST_ROWS, 8)
            sources = snd[pl.ds(base + 32, 8), :].astype(jnp.int32)
            slots = snd[pl.ds(base + 40, 8), :].astype(jnp.int32)
            live = slots >= 0
            group = jnp.where(live, lax.shift_right_arithmetic(slots, 7), 0)
            factor = jnp.where(live, jnp.take_along_axis(own_table, group, axis=1), 0.0)
            high = lax.shift_right_arithmetic(sources, 7)
            low = lax.bitwise_and(sources, 127)
            for t in range(4):
                picked = jnp.zeros((8, 128), F32)
                for h in range(8):
                    row = jnp.broadcast_to(cland[slab, 8 * t + h:8 * t + h + 1, :], (8, 128))
                    picked = jnp.where(high == h, jnp.take_along_axis(row, low, axis=1), picked)
                old = snd[pl.ds(base + 8 * t, 8), :]
                fresh = (jnp.where(live, old, 0.0) + STEP * jnp.where(live, picked, 0.0)) * factor
                lat_out[t, pl.ds(pl.multiple_of(8 * slab, 8), 8), :] = fresh
        return carry

    lax.fori_loop(0, n_var // 2, renew, 0)

    drain(pland.at[pl.ds(0, n_var - 1)], recv_sems.at[6])
    predicted = pland[0]
    for k in range(1, n_var):
        predicted = predicted + pland[k]
    for k in range(lanes):
        res_out[:, 128 * k:128 * (k + 1)] = residual[:, 128 * k:128 * (k + 1)] - predicted[4 * k:4 * k + 4, :] * inverse_root

    drain(halves, send_sems.at[0])
    drain(spc, send_sems.at[9])
    drain(win.at[pl.ds(0, 2 * reach - 1)], send_sems.at[1])
    drain(gland.at[pl.ds(0, n_var - 1)], send_sems.at[3])
    drain(cpart, send_sems.at[4])
    drain(cland.at[pl.ds(0, n_var - 1), own_rows, :], send_sems.at[5])
    drain(cland.at[:, own_rows, :], send_sems.at[8])
    drain(pland.at[pl.ds(0, n_var - 1)], send_sems.at[6])

    @pl.when(active)
    def _():
        drain(snd.at[pl.ds(0, LIST_ROWS * (n_var - 1)), :], send_sems.at[2])
        drain(own, send_sems.at[7])


def hand_out(lat, coef, res, lat_out, coef_out, res_out, sems):
    copies = [pltpu.make_async_copy(src, dst, sems.at[k])
              for k, (src, dst) in enumerate(((lat, lat_out), (coef, coef_out), (res, res_out)))]
    for copy in copies:
        copy.start()
    for copy in copies:
        copy.wait()


def per_device(n_people, n_var, genotype, dosage_mean, residual, latent_old, group_weight, copy_source, copy_slot):
    people_dev, var_dev = genotype.shape
    traits = residual.shape[0]
    inverse_root = 1.0 / math.sqrt(people_dev * n_people)
    half = n_var // 2
    n_z = n_people // 2
    list_rows = n_var * var_dev // 128
    vmem = pl.BlockSpec(memory_space=pltpu.VMEM)
    hbm = pl.BlockSpec(memory_space=pltpu.HBM)
    shapes = ((traits, list_rows, 128), (traits, var_dev), (traits, people_dev))
    held = pl.pallas_call(
        functools.partial(kernel, n_people, n_var, inverse_root),
        out_shape=tuple(pltpu.VMEM(shape, F32) for shape in shapes),
        in_specs=[hbm] * 7,
        out_specs=(vmem,) * 3,
        scratch_shapes=[
            pltpu.VMEM((people_dev, var_dev), jnp.int32),
            pltpu.VMEM((people_dev, var_dev), BF16),
            pltpu.VMEM((1, var_dev), F32),
            pltpu.VMEM((traits, people_dev), F32),
            pltpu.VMEM((traits, list_rows, 128), F32),
            pltpu.VMEM((1, 128), F32),
            pltpu.VMEM((n_var, 1024), jnp.int32),
            pltpu.VMEM((n_var, 1024), jnp.int32),
            pltpu.VMEM((n_var * LIST_ROWS, 128), F32),
            pltpu.VMEM((half, LIST_ROWS, 128), F32),
            pltpu.VMEM((32, 128), F32),
            pltpu.VMEM((16, 128), F32),
            pltpu.VMEM((n_z // 2, 16, 128), F32),
            pltpu.VMEM((16, 128), F32),
            pltpu.VMEM((2, 32, 128), F32),
            pltpu.VMEM((32, 128), F32),
            pltpu.VMEM((32, 8, 128), F32),
            pltpu.VMEM((half * 128, 1024), BF16),
            pltpu.VMEM((half * 1024, 128), BF16),
            pltpu.VMEM((half * 8, 8, 128), F32),
            pltpu.VMEM((half, 32, 128), F32),
            pltpu.VMEM((half, 32, 128), F32),
            pltpu.VMEM((half * 8, 128), F32),
            pltpu.VMEM((n_var, half, 128), F32),
            pltpu.VMEM((half, 128), F32),
            pltpu.VMEM((64, half * 1024), BF16),
            pltpu.VMEM((n_var, 32, 128), F32),
            pltpu.VMEM((1, 128), F32),
            pltpu.VMEM((32, 128), F32),
            pltpu.VMEM((32, 128), F32),
            pltpu.VMEM((32, 128), F32),
            pltpu.VMEM((n_var, people_dev // 32, 128), F32),
            pltpu.VMEM((people_dev // 32, 128), F32),
            pltpu.SemaphoreType.DMA((10,)),
            pltpu.SemaphoreType.DMA((10,)),
            pltpu.SemaphoreType.DMA((10,)),
        ],
        compiler_params=pltpu.CompilerParams(collective_id=0, has_side_effects=True, vmem_limit_bytes=32 * 2**20),
    )(*(pltpu.with_memory_space_constraint(x, pltpu.HBM) for x in (
        genotype,
        dosage_mean.reshape(1, var_dev),
        residual,
        latent_old.reshape(traits, list_rows, 128),
        group_weight.reshape(1, 128),
        copy_source[0],
        copy_slot[0],
    )))
    lat, coef, res = pl.pallas_call(
        hand_out,
        out_shape=tuple(jax.ShapeDtypeStruct(shape, F32) for shape in shapes),
        in_specs=[vmem] * 3,
        out_specs=(hbm,) * 3,
        scratch_shapes=[pltpu.SemaphoreType.DMA((3,))],
    )(*(pltpu.with_memory_space_constraint(x, pltpu.VMEM) for x in held))
    return lat.reshape(latent_old.shape), coef, res


def solution(mesh):
    return jax.shard_map(
        functools.partial(per_device, mesh.shape["people"], mesh.shape["var"]),
        mesh=mesh,
        in_specs=(
            P("people", "var"),
            P("var"),
            P(None, "people"),
            P(None, "var", None),
            P("var"),
            P("var", None, None),
            P("var", None, None),
        ),
        out_specs=(P(None, "var", None), P(None, "var"), P(None, "people")),
        check_vma=False,
    )
```
